768 devices in a mesh: blk: 384 (over x, z, y), rep: 2 (over core).
Axes of the slice: x: 4, y: 8, z: 12, core: 2. Of those that a mesh axis runs over, the one named last changes fastest.
Arguments:
- features: bfloat16 [786432, 256], P('blk', 'rep'), may hold values from -0.0068359375 to 0.0068359375
- out_grad: bfloat16 [786432, 256], P('blk', 'rep'), may hold values from -6 to 6
- block_tiles: bfloat16 [24576, 128, 128], P('blk'), may hold values from -0.25 to 0.25
- block_cols: int32 [24576], P('blk'), may hold values from 0 to 6143, as said below
- self_weight: bfloat16 [256, 256], P('rep'), may hold values from -0.375 to 0.375
- neighbor_weight: bfloat16 [256, 256], P('rep'), may hold values from -0.375 to 0.375
Outputs:
- feature_grad: float32 [786432, 256], P('blk', 'rep')
- self_weight_grad: float32 [256, 256], P('rep')
- neighbor_weight_grad: float32 [256, 256], P('rep')
The draws below stay inside these ranges and needn't reach their ends.
Inputs may be any that keep to these rules, and one draw needn't show every extreme that they name: `block_cols`: slots m * 64 to (m + 1) * 64 - 1 hold the tiles of row blocks m * 16 to (m + 1) * 16 - 1 (range m). Every tile names a column block of its own range, except the first tile of row block m * 16 + b: for b < 2 it names block 15 - b of range m - 1, for b >= 14 block 15 - b of range m + 1, where range -1 is the last range and the range after the last is range 0.
All inputs are finite; a program needn't handle non-finite values.
Results may differ from the reference program's by a relative error of at most 0.0031.
Values may be sent and summed in bfloat16 or wider, within the bound.
A program may use at most 32 MiB of HBM per device.

```python
import jax
import jax.numpy as jnp
from jax import lax

H = 256
BLOCK = 128
PER_BLOCK = 4
HALO = 2
BLK_DEV = 16
TILE_DEV = 64
NODE_BLOCKS = 6144
NODES = 786432
TILES = 24576


def draw_block_cols(key, part):
    key = jax.random.fold_in(key, 11)
    ranges = NODE_BLOCKS // BLK_DEV
    slot = jnp.arange(TILES, dtype=jnp.int32)
    owner = slot // TILE_DEV
    row_block = slot % TILE_DEV // PER_BLOCK
    leading = slot % PER_BLOCK == 0
    chosen = jax.random.randint(key, (TILES,), 0, BLK_DEV, dtype=jnp.int32)
    inside = owner * BLK_DEV + chosen
    mirror = BLK_DEV - 1 - row_block
    before = (owner + ranges - 1) % ranges * BLK_DEV + mirror
    after = (owner + 1) % ranges * BLK_DEV + mirror
    result = jnp.where(leading & (row_block < HALO), before, jnp.where(leading & (row_block >= BLK_DEV - HALO), after, inside))
    return result.astype(jnp.int32)


def block_scale(rng, dims, split, low, top_value):
    loudness = 1.0
    for position, parts in split:
        heights = jax.random.uniform(jax.random.fold_in(jax.random.fold_in(rng, 6), position), (parts,), jnp.float32, low / len(split), top_value / len(split))
        loudness = loudness * jnp.repeat(jnp.exp(heights), dims[position] // parts).reshape((-1,) + (1,) * (len(dims) - 1 - position))
    return loudness


def normal_values(key, dims, width, most, pieces=(), kind=jnp.bfloat16):
    drawn = jax.random.normal(key, dims, jnp.float32) * width
    if len(pieces) > 0:
        drawn = block_scale(key, dims, pieces, -0.22, 0.18) * drawn
    return jnp.clip(drawn, min=-most, max=most).astype(kind)


def setup_inputs(seed: int = 0) -> dict:
    key_list = jax.random.split(jax.random.key(seed), 7)
    return {
        "features": normal_values(key_list[0], (NODES, H), NODES ** -0.5, 0.0068359375, ((0, 384), (1, 2))),
        "out_grad": normal_values(key_list[1], (NODES, H), 1.0, 6.0, ((0, 384), (1, 2))),
        "block_tiles": normal_values(key_list[2], (TILES, BLOCK, BLOCK), (BLOCK * PER_BLOCK) ** -0.5, 0.25, ((0, 384),)),
        "block_cols": draw_block_cols(jax.random.fold_in(key_list[6], 71), 0),
        "self_weight": normal_values(key_list[4], (H, H), H ** -0.5, 0.375, ((0, 2),)),
        "neighbor_weight": normal_values(key_list[5], (H, H), H ** -0.5, 0.375, ((0, 2),)),
    }


def reference(features, out_grad, block_tiles, block_cols, self_weight, neighbor_weight):
    ranges = NODE_BLOCKS // BLK_DEV
    feat_blocks = features.reshape(NODE_BLOCKS, BLOCK, H)
    projected = jnp.dot(out_grad, neighbor_weight.T, preferred_element_type=jnp.float32).astype(jnp.bfloat16)
    proj_blocks = projected.reshape(NODE_BLOCKS, BLOCK, H)
    tile_ranges = block_tiles.reshape(ranges, TILE_DEV, BLOCK, BLOCK)
    col_ranges = block_cols.reshape(ranges, TILE_DEV)

    def aggregate_range(index):
        tile_part = tile_ranges[index].astype(jnp.float32)
        picked = jnp.take(feat_blocks, col_ranges[index], axis=0).astype(jnp.float32)
        summed = jnp.einsum("tij,tjk->tik", tile_part, picked)
        return summed.reshape(BLK_DEV, PER_BLOCK, BLOCK, H).sum(axis=1).astype(jnp.bfloat16)

    aggregate = lax.map(aggregate_range, jnp.arange(ranges, dtype=jnp.int32)).reshape(NODES, H)

    def scatter_range(carry, index):
        tile_part = tile_ranges[index].astype(jnp.float32).reshape(BLK_DEV, PER_BLOCK, BLOCK, BLOCK)
        row_part = lax.dynamic_slice_in_dim(proj_blocks, (index * BLK_DEV).astype(jnp.int32), BLK_DEV, 0).astype(jnp.float32)
        terms = jnp.einsum("bpij,bik->bpjk", tile_part, row_part).reshape(TILE_DEV, BLOCK, H)
        return carry.at[col_ranges[index]].add(terms), None

    neighbor_term, unused = lax.scan(scatter_range, jnp.zeros((NODE_BLOCKS, BLOCK, H), jnp.float32), jnp.arange(ranges, dtype=jnp.int32))
    self_term = jnp.dot(out_grad, self_weight.T, preferred_element_type=jnp.float32)
    feature_grad = self_term + neighbor_term.reshape(NODES, H)
    self_weight_grad = jnp.dot(features.T, out_grad, preferred_element_type=jnp.float32)
    neighbor_weight_grad = jnp.dot(aggregate.T, out_grad, preferred_element_type=jnp.float32)
    return (feature_grad, self_weight_grad, neighbor_weight_grad)
```

```python
import functools

import jax
import jax.numpy as jnp
from jax import lax
from jax.experimental import pallas as pl
from jax.experimental.pallas import tpu as pltpu
from jax.sharding import PartitionSpec as P

HALO = 2
SIDE = 128
TORUS = (4, 12, 8)
CHUNKS = 4
BF16, F32 = jnp.bfloat16, jnp.float32


def dot(a, b):
    return jnp.dot(a, b, preferred_element_type=F32)


def kernel(
    torus,
    feat, grad, tiles, cols, self_w, neigh_w,
    fgrad, wgrad,
    tile_buf, feat_buf, grad_buf, w_buf, cols_v, index_v, index_s,
    chain, full_t, ext_hi, ext_lo, rim_out, rim_in, fg_buf,
    part, got_x, sum_x, got_y, sum_y, got_z, all_y, all_x, w_out,
    load_sem, tile_sem, out_sem, pair_send, pair_recv, rim_send, rim_recv,
    send_x, recv_x, send_y, recv_y, send_z, recv_z, send_ay, recv_ay, send_ax, recv_ax,
):
    nx, nz, ny = torus
    n = nx * nz * ny
    m, c = lax.axis_index("blk"), lax.axis_index("rep")
    x, z, y = m // (nz * ny), (m // ny) % nz, m % ny
    rows = grad.shape[0]
    blocks = rows // SIDE
    ext = blocks + 2 * HALO
    per = tiles.shape[0] // blocks
    rim = HALO * SIDE
    up, down = (m + 1) % n, (m + n - 1) % n
    other = 1 - c

    def at(xx, zz, yy):
        return (xx * nz + zz) * ny + yy

    group_x = [((x + k // 2) % nx, (c + k % 2) % 2) for k in range(1, 2 * nx)]
    group_y = [(y + k) % ny for k in range(1, ny)]
    group_z = [(z + k) % nz for k in range(1, nz)]
    group_ax = [(x + k) % nx for k in range(1, nx)]

    def remote(src, dst, send, recv, blk, rep):
        return pltpu.make_async_remote_copy(
            src_ref=src, dst_ref=dst, send_sem=send, recv_sem=recv,
            device_id={"blk": blk, "rep": rep}, device_id_type=pl.DeviceIdType.MESH,
        )

    own_cols = pl.ds(pl.multiple_of(c * SIDE, SIDE), SIDE)
    loads = [
        pltpu.make_async_copy(cols, cols_v, load_sem.at[0]),
        pltpu.make_async_copy(grad, grad_buf, load_sem.at[1]),
    ]
    chunk = tiles.shape[0] // CHUNKS
    tile_loads = [
        pltpu.make_async_copy(tiles.at[pl.ds(i * chunk, chunk)], tile_buf.at[pl.ds(i * chunk, chunk)], tile_sem.at[i])
        for i in range(CHUNKS)
    ]
    late_loads = [
        pltpu.make_async_copy(feat, feat_buf.at[pl.ds(rim, rows), own_cols], load_sem.at[2]),
        pltpu.make_async_copy(self_w, w_buf.at[0], load_sem.at[3]),
        pltpu.make_async_copy(neigh_w, w_buf.at[1], load_sem.at[4]),
    ]
    for copy in loads + tile_loads + late_loads:
        copy.start()

    barrier = pltpu.get_barrier_semaphore()
    peers = [(at(xx, z, y), cc) for xx, cc in group_x]
    peers += [(at(x, z, yy), c) for yy in group_y]
    peers += [(at(x, zz, y), c) for zz in group_z]
    peers += [(blk, rep) for blk in (up, down) for rep in (c, other)]
    for blk, rep in peers:
        pl.semaphore_signal(barrier, inc=1, device_id={"blk": blk, "rep": rep}, device_id_type=pl.DeviceIdType.MESH)

    loads[0].wait()
    count = tiles.shape[0]
    slot = cols_v[...] - m * blocks + HALO
    slot = jnp.where(slot < 0, slot + n * blocks, slot)
    slot = jnp.where(slot >= n * blocks, slot - n * blocks, slot)
    slot = jnp.concatenate([slot, jnp.full((1, SIDE - count), -1, jnp.int32)], axis=1)
    across = jnp.broadcast_to(slot, (SIDE, SIDE))
    along = across.T
    row = lax.broadcasted_iota(jnp.int32, (SIDE, SIDE), 0)
    lane = lax.broadcasted_iota(jnp.int32, (SIDE, SIDE), 1)
    before = jnp.max(jnp.where((across == along) & (row < lane), row, -1), axis=0, keepdims=True)
    final = jnp.max(jnp.where((along == lane) & (row < count), row, -1), axis=0, keepdims=True)
    index_v[0:1, :] = jnp.where(before < 0, count, before)
    index_v[1:2, :] = jnp.where(final < 0, count, final)
    to_scalar = pltpu.make_async_copy(index_v, index_s, load_sem.at[5])
    to_scalar.start()
    chain[count] = jnp.zeros((SIDE, SIDE), F32)
    to_scalar.wait()

    pl.semaphore_wait(barrier, len(peers))
    pair_feat = remote(feat, feat_buf.at[pl.ds(rim, rows), own_cols], pair_send.at[0], pair_recv.at[0], m, other)
    pair_feat.start()
    rims = []
    for k, rep in enumerate((c, other)):
        rims.append(remote(
            feat.at[pl.ds(0, rim)], feat_buf.at[pl.ds(rim + rows, rim), own_cols],
            rim_send.at[k], rim_recv.at[k], down, rep))
        rims.append(remote(
            feat.at[pl.ds(rows - rim, rim)], feat_buf.at[pl.ds(0, rim), own_cols],
            rim_send.at[2 + k], rim_recv.at[2 + k], up, rep))
    for copy in rims:
        copy.start()

    loads[1].wait()
    for i in range(CHUNKS):
        tile_loads[i].wait()

        def row_block(b, carry):
            span = pl.ds(pl.multiple_of(b * SIDE, SIDE), SIDE)
            g_t = grad_buf[span, :].T
            full_t[c, :, span] = g_t
            side = jnp.concatenate([tile_buf[b * per + k] for k in range(per)], axis=1)
            product = dot(g_t, side)
            for k in range(per):
                t = b * per + k
                chain[t] = chain[index_s[0, t]] + product[:, k * SIDE:(k + 1) * SIDE]
            return carry

        step = blocks // CHUNKS
        lax.fori_loop(i * step, (i + 1) * step, row_block, 0)

    pair_grad = remote(full_t.at[c], full_t.at[c], pair_send.at[1], pair_recv.at[1], m, other)
    pair_grad.start()
    for k in range(ext):
        span = pl.ds(k * SIDE, SIDE)
        value = chain[index_s[1, k]]
        hi = value.astype(BF16)
        ext_hi[:, span] = hi
        ext_lo[:, span] = (value - hi.astype(F32)).astype(BF16)
        if k < HALO:
            rim_out[0, k] = value
        elif k >= ext - HALO:
            rim_out[1, k - ext + HALO] = value
        elif 2 * HALO <= k < ext - 2 * HALO:
            full_t[2 + c, :, pl.ds((k - HALO) * SIDE, SIDE)] = hi
    sums = [
        remote(rim_out.at[0], rim_in.at[0], rim_send.at[4], rim_recv.at[4], down, c),
        remote(rim_out.at[1], rim_in.at[1], rim_send.at[5], rim_recv.at[5], up, c),
    ]
    for copy in sums:
        copy.start()

    late_loads[0].wait()
    pair_feat.wait_recv()
    share = SIDE // nx

    def put(which, value):
        for r in range(2):
            for q in range(nx):
                part[r, q, which * share:(which + 1) * share, :] = (
                    value[q * share:(q + 1) * share, r * SIDE:(r + 1) * SIDE])

    put(0, dot(full_t[c], feat_buf[rim:rim + rows, :]))
    for copy in rims:
        copy.wait_recv()
    every = feat_buf[...]
    put(1, dot(ext_hi[...], every) + dot(ext_lo[...], every))

    stage_x = []
    for xx, cc in group_x:
        stage_x.append(remote(
            part.at[cc, xx], got_x.at[2 * x + c], send_x.at[2 * xx + cc], recv_x.at[2 * x + c], at(xx, z, y), cc))
        stage_x[-1].start()

    for copy in sums:
        copy.wait_recv()
    for k in range(2 * HALO):
        low = k < HALO
        b = k if low else blocks - 2 * HALO + k
        span = pl.ds(b * SIDE, SIDE)
        value = chain[index_s[1, b + HALO]] + (rim_in[1, k] if low else rim_in[0, k - HALO])
        full_t[2 + c, :, span] = value.astype(BF16)
    pair_sum = remote(full_t.at[2 + c], full_t.at[2 + c], pair_send.at[2], pair_recv.at[2], m, other)
    pair_sum.start()

    got_x[2 * x + c] = part[c, x]
    for xx, cc in group_x:
        s = 2 * xx + cc
        pltpu.make_async_copy(part.at[c, x], got_x.at[s], recv_x.at[s]).wait()
    for cc in range(2):
        total = got_x[cc]
        for xx in range(1, nx):
            total = total + got_x[2 * xx + cc]
        sum_x[cc * 2 * share:(cc + 1) * 2 * share, :] = total

    piece = 4 * share // ny
    stage_y = []
    for yy in group_y:
        stage_y.append(remote(
            sum_x.at[pl.ds(pl.multiple_of(yy * piece, piece), piece)], got_y.at[y],
            send_y.at[yy], recv_y.at[y], at(x, z, yy), c))
        stage_y[-1].start()

    for copy in late_loads[1:]:
        copy.wait()
    pair_grad.wait_recv()
    pair_sum.wait_recv()
    weights = jnp.concatenate([w_buf[0], w_buf[1]], axis=1)
    wide = 2 * SIDE

    def feature_part(i, carry):
        span = pl.ds(pl.multiple_of(i * wide, wide), wide)
        fg_buf[span, :] = dot(weights, full_t[:, :, span].reshape(4 * SIDE, wide)).T
        return carry

    halves = rows // wide // 2
    lax.fori_loop(0, halves, feature_part, 0)
    outs = [
        pltpu.make_async_copy(
            fg_buf.at[pl.ds(i * (rows // 2), rows // 2)], fgrad.at[pl.ds(i * (rows // 2), rows // 2)], out_sem.at[i])
        for i in range(2)
    ]
    outs[0].start()

    got_y[y] = sum_x[pl.ds(pl.multiple_of(y * piece, piece), piece), :]
    for yy in group_y:
        pltpu.make_async_copy(sum_y, got_y.at[yy], recv_y.at[yy]).wait()
    total = got_y[0]
    for yy in range(1, ny):
        total = total + got_y[yy]
    sum_y[...] = total

    stage_z = []
    for zz in group_z:
        stage_z.append(remote(sum_y, got_z.at[z], send_z.at[zz], recv_z.at[z], at(x, zz, y), c))
        stage_z[-1].start()
    lax.fori_loop(halves, 2 * halves, feature_part, 0)
    outs[1].start()

    got_z[z] = total
    for zz in group_z:
        pltpu.make_async_copy(sum_y, got_z.at[zz], recv_z.at[zz]).wait()
    total = got_z[0]
    for zz in range(1, nz):
        total = total + got_z[zz]
    own_piece = pl.ds(pl.multiple_of(y * piece, piece), piece)
    all_y[own_piece, :] = total

    back_y = []
    for yy in group_y:
        back_y.append(remote(all_y.at[own_piece], all_y.at[own_piece], send_ay.at[yy], recv_ay.at[y], at(x, z, yy), c))
        back_y[-1].start()
    for yy in group_y:
        other_piece = pl.ds(pl.multiple_of(yy * piece, piece), piece)
        pltpu.make_async_copy(all_y.at[own_piece], all_y.at[other_piece], recv_ay.at[yy]).wait()
    back_x = []
    for xx in group_ax:
        back_x.append(remote(all_y, all_x.at[x], send_ax.at[xx], recv_ax.at[x], at(xx, z, y), c))
        back_x[-1].start()
    all_x[x] = all_y[...]
    for xx in group_ax:
        pltpu.make_async_copy(all_y, all_x.at[xx], recv_ax.at[xx]).wait()
    for which in range(2):
        for cc in range(2):
            base = (2 * cc + which) * share
            value = jnp.concatenate([all_x[q, base:base + share, :] for q in range(nx)], axis=0)
            w_out[which, :, cc * SIDE:(cc + 1) * SIDE] = value.T
    last = pltpu.make_async_copy(w_out, wgrad, out_sem.at[2])
    last.start()

    for copy in [pair_feat, pair_grad, pair_sum] + rims + sums + stage_x + stage_y + stage_z + back_y + back_x:
        copy.wait_send()
    for copy in outs:
        copy.wait()
    last.wait()


def body(torus, features, out_grad, block_tiles, block_cols, self_weight, neighbor_weight):
    nx, nz, ny = torus
    rows, columns = features.shape
    width = self_weight.shape[1]
    count = block_tiles.shape[0]
    blocks = rows // SIDE
    ext = blocks + 2 * HALO
    share = SIDE // nx
    piece = 4 * share // ny
    dma = pltpu.SemaphoreType.DMA
    anywhere = pl.BlockSpec(memory_space=pl.ANY)
    feature_grad, weight_grad = pl.pallas_call(
        functools.partial(kernel, torus),
        out_shape=(
            jax.ShapeDtypeStruct((rows, columns), F32),
            jax.ShapeDtypeStruct((2, columns, width), F32),
        ),
        in_specs=[anywhere] * 6,
        out_specs=(anywhere, anywhere),
        scratch_shapes=[
            pltpu.VMEM((count, SIDE, SIDE), BF16),
            pltpu.VMEM((ext * SIDE, 2 * SIDE), BF16),
            pltpu.VMEM((rows, columns), BF16),
            pltpu.VMEM((2, SIDE, width), BF16),
            pltpu.VMEM((1, count), jnp.int32),
            pltpu.VMEM((8, SIDE), jnp.int32),
            pltpu.SMEM((8, SIDE), jnp.int32),
            pltpu.VMEM((count + 1, SIDE, SIDE), F32),
            pltpu.VMEM((4, SIDE, rows), BF16),
            pltpu.VMEM((SIDE, ext * SIDE), BF16),
            pltpu.VMEM((SIDE, ext * SIDE), BF16),
            pltpu.VMEM((2, HALO, SIDE, SIDE), F32),
            pltpu.VMEM((2, HALO, SIDE, SIDE), F32),
            pltpu.VMEM((rows, columns), F32),
            pltpu.VMEM((2, nx, 2 * share, SIDE), F32),
            pltpu.VMEM((2 * nx, 2 * share, SIDE), F32),
            pltpu.VMEM((4 * share, SIDE), F32),
            pltpu.VMEM((ny, piece, SIDE), F32),
            pltpu.VMEM((piece, SIDE), F32),
            pltpu.VMEM((nz, piece, SIDE), F32),
            pltpu.VMEM((4 * share, SIDE), F32),
            pltpu.VMEM((nx, 4 * share, SIDE), F32),
            pltpu.VMEM((2, columns, width), F32),
            dma((6,)), dma((CHUNKS,)), dma((3,)), dma((3,)), dma((3,)), dma((6,)), dma((6,)),
            dma((2 * nx,)), dma((2 * nx,)), dma((ny,)), dma((ny,)), dma((nz,)), dma((nz,)),
            dma((ny,)), dma((ny,)), dma((nx,)), dma((nx,)),
        ],
        compiler_params=pltpu.CompilerParams(
            collective_id=0, has_side_effects=True, vmem_limit_bytes=40 * 1024 * 1024
        ),
        cost_estimate=pl.CostEstimate(flops=1100000000, bytes_accessed=4500000, transcendentals=0),
    )(features, out_grad, block_tiles, block_cols.reshape(1, count), self_weight, neighbor_weight)
    return feature_grad, weight_grad[0], weight_grad[1]


def solution(mesh):
    in_specs = (
        P("blk", "rep"),
        P("blk", "rep"),
        P("blk", None, None),
        P("blk"),
        P("rep", None),
        P("rep", None),
    )
    out_specs = (P("blk", "rep"), P("rep", None), P("rep", None))
    step = functools.partial(body, TORUS)
    return jax.shard_map(step, mesh=mesh, in_specs=in_specs, out_specs=out_specs, check_vma=False)
```

```python
import functools

import jax
import jax.numpy as jnp
from jax import lax
from jax.experimental import pallas as pl
from jax.experimental.pallas import tpu as pltpu
from jax.sharding import PartitionSpec as P

HALO = 2
SIDE = 128
TORUS = (4, 12, 8)
CHUNKS = 4
VMEM_BYTES = 60 * 1024 * 1024
BF16, F32 = jnp.bfloat16, jnp.float32


def dot(a, b):
    return jnp.dot(a, b, preferred_element_type=F32)


def kernel(
    torus,
    feat, grad, tiles, cols, self_w, neigh_w,
    fgrad, wgrad,
    tile_buf, feat_buf, grad_buf, w_buf, cols_v, index_v, index_s,
    chain, full_t, low_t, rim_out, rim_in,
    part, got_x, sum_x, got_y, sum_y, got_z, every,
    load_sem, tile_sem, pair_send, pair_recv, rim_send, rim_recv,
    send_x, recv_x, send_y, recv_y, send_z, recv_z, send_ay, recv_ay, send_ax, recv_ax,
):
    nx, nz, ny = torus
    n = nx * nz * ny
    m, c = lax.axis_index("blk"), lax.axis_index("rep")
    x, z, y = m // (nz * ny), (m // ny) % nz, m % ny
    rows = grad.shape[0]
    blocks = rows // SIDE
    count = tiles.shape[0]
    per = count // blocks
    up, down = (m + 1) % n, (m + n - 1) % n
    other = 1 - c

    def at(xx, zz, yy):
        return (xx * nz + zz) * ny + yy

    def far_first(size):
        return sorted(range(1, size), key=lambda k: -min(k, size - k))

    group_x = [((x + k) % nx, (c + j) % 2) for k in far_first(nx) + [0] for j in ((0, 1) if k else (1,))]
    group_y = [(y + k) % ny for k in far_first(ny)]
    group_z = [(z + k) % nz for k in far_first(nz)]
    group_ax = [(x + k) % nx for k in far_first(nx)]

    def remote(src, dst, send, recv, blk, rep):
        return pltpu.make_async_remote_copy(
            src_ref=src, dst_ref=dst, send_sem=send, recv_sem=recv,
            device_id={"blk": blk, "rep": rep}, device_id_type=pl.DeviceIdType.MESH,
        )

    def arrived(like, recv):
        pltpu.make_async_copy(like, like, recv).wait()

    barrier = pltpu.get_barrier_semaphore()
    peers = [(at(x, zz, y), c) for zz in group_z]
    peers += [(at(x, z, yy), c) for yy in group_y]
    peers += [(at(xx, z, y), cc) for xx, cc in group_x]
    peers += [(up, c), (down, c)]
    for blk, rep in peers:
        pl.semaphore_signal(barrier, inc=1, device_id={"blk": blk, "rep": rep}, device_id_type=pl.DeviceIdType.MESH)

    own_cols = pl.ds(pl.multiple_of(c * SIDE, SIDE), SIDE)
    first_loads = [
        pltpu.make_async_copy(cols, cols_v, load_sem.at[0]),
        pltpu.make_async_copy(grad, grad_buf, load_sem.at[1]),
    ]
    chunk = count // CHUNKS
    order = [0, CHUNKS - 1] + list(range(1, CHUNKS - 1))
    tile_loads = {
        i: pltpu.make_async_copy(tiles.at[pl.ds(i * chunk, chunk)], tile_buf.at[pl.ds(i * chunk, chunk)], tile_sem.at[i])
        for i in order
    }
    late_loads = [
        pltpu.make_async_copy(feat, feat_buf.at[:, own_cols], load_sem.at[2]),
        pltpu.make_async_copy(self_w, w_buf.at[0], load_sem.at[3]),
        pltpu.make_async_copy(neigh_w, w_buf.at[1], load_sem.at[4]),
    ]
    for copy in first_loads + [tile_loads[i] for i in order] + late_loads:
        copy.start()

    ahead = {0: 0, CHUNKS - 1: (2 - CHUNKS) * chunk} | {i: chunk for i in range(1, CHUNKS - 1)}

    def place(t):
        return jnp.where(t < chunk, t, jnp.where(t >= count - chunk, t + ahead[CHUNKS - 1], t + chunk))

    first_loads[0].wait()
    slot = cols_v[...] - m * blocks
    slot = jnp.concatenate([slot, jnp.full((1, SIDE - count), -1, jnp.int32)], axis=1)
    across = jnp.broadcast_to(slot, (SIDE, SIDE))
    along = across.T
    row = lax.broadcasted_iota(jnp.int32, (SIDE, SIDE), 0)
    lane = lax.broadcasted_iota(jnp.int32, (SIDE, SIDE), 1)
    row_at, lane_at = place(row), place(lane)
    before = jnp.max(jnp.where((across == along) & (row_at < lane_at), row_at, -1), axis=0, keepdims=True)
    final = jnp.max(jnp.where((along == lane) & (row < count), row_at, -1), axis=0, keepdims=True)
    index_v[0:1, :] = jnp.where(before < 0, count, before)
    index_v[1:2, :] = jnp.where(final < 0, count, final)
    to_scalar = pltpu.make_async_copy(index_v, index_s, load_sem.at[5])
    to_scalar.start()
    chain[count] = jnp.zeros((SIDE, SIDE), F32)
    to_scalar.wait()

    def row_block(shift, b, carry):
        span = pl.ds(pl.multiple_of(b * SIDE, SIDE), SIDE)
        g_t = grad_buf[span, :].T
        full_t[c, :, span] = g_t
        product = dot(g_t, jnp.concatenate([tile_buf[b * per + k] for k in range(per)], axis=1))
        for k in range(per):
            t = b * per + k
            chain[t + shift] = chain[index_s[0, t]] + product[:, k * SIDE:(k + 1) * SIDE]
        return carry

    def tile_work(i):
        tile_loads[i].wait()
        step = blocks // CHUNKS
        lax.fori_loop(i * step, (i + 1) * step, functools.partial(row_block, ahead[i]), 0)

    first_loads[1].wait()
    for i in order[:2]:
        tile_work(i)
    for k in range(HALO):
        rim_out[0, k] = chain[k * per].astype(BF16)
        rim_out[1, k] = chain[(blocks - HALO + k) * per + ahead[CHUNKS - 1]].astype(BF16)

    pl.semaphore_wait(barrier, len(peers))
    sums = [
        remote(rim_out.at[0], rim_in.at[0], rim_send.at[0], rim_recv.at[0], down, c),
        remote(rim_out.at[1], rim_in.at[1], rim_send.at[1], rim_recv.at[1], up, c),
    ]
    for copy in sums:
        copy.start()
    pair_feat = remote(feat, feat_buf.at[:, own_cols], pair_send.at[0], pair_recv.at[0], m, other)
    pair_feat.start()
    for i in order[2:]:
        tile_work(i)

    def column_block(b, value):
        span = pl.ds(b * SIDE, SIDE)
        hi = value.astype(BF16)
        full_t[2 + c, :, span] = hi
        low_t[:, span] = (value - hi.astype(F32)).astype(BF16)

    for b in range(HALO, blocks - HALO):
        column_block(b, chain[index_s[1, b]])

    share = SIDE // nx
    stage_x = [[], []]

    def send_share(which, value):
        for r in range(2):
            for q in range(nx):
                part[which, r, q] = value[q * share:(q + 1) * share, r * SIDE:(r + 1) * SIDE]
        for xx, cc in group_x:
            stage_x[which].append(remote(
                part.at[which, cc, xx], got_x.at[which, 2 * x + c],
                send_x.at[which, 2 * xx + cc], recv_x.at[which, 2 * x + c], at(xx, z, y), cc))
            stage_x[which][-1].start()
        got_x[which, 2 * x + c] = part[which, c, x]

    late_loads[0].wait()
    pair_feat.wait_recv()
    send_share(0, dot(full_t[c], feat_buf[...]))
    for copy in sums:
        copy.wait_recv()
    for k in range(HALO):
        b = blocks - 1 - k
        column_block(b, chain[index_s[1, b]] + rim_in[0, k].astype(F32))
        b = HALO - 1 - k
        column_block(b, chain[index_s[1, b]] + rim_in[1, k].astype(F32))
    send_share(1, dot(full_t[2 + c], feat_buf[...]) + dot(low_t[...], feat_buf[...]))
    pair_grad = remote(full_t.at[c], full_t.at[c], pair_send.at[1], pair_recv.at[1], m, other)
    pair_grad.start()
    pair_sum = remote(full_t.at[2 + c], full_t.at[2 + c], pair_send.at[2], pair_recv.at[2], m, other)
    pair_sum.start()
    for copy in late_loads[1:]:
        copy.wait()

    for which in range(2):
        for xx, cc in group_x:
            arrived(part.at[which, c, x], recv_x.at[which, 2 * xx + cc])
        for cc in range(2):
            total = got_x[which, cc]
            for xx in range(1, nx):
                total = total + got_x[which, 2 * xx + cc]
            sum_x[(2 * cc + which) * share:(2 * cc + which + 1) * share, :] = total

    piece = 4 * share // ny
    own_piece = pl.ds(pl.multiple_of(y * piece, piece), piece)
    stage_y = []
    for yy in group_y:
        stage_y.append(remote(
            sum_x.at[pl.ds(pl.multiple_of(yy * piece, piece), piece)], got_y.at[y],
            send_y.at[yy], recv_y.at[y], at(x, z, yy), c))
        stage_y[-1].start()
    got_y[y] = sum_x[own_piece, :]

    pair_grad.wait_recv()
    pair_sum.wait_recv()
    weights = jnp.concatenate([w_buf[0], w_buf[1]], axis=1)
    wide = 2 * SIDE

    def feature_part(i, carry):
        span = pl.ds(pl.multiple_of(i * wide, wide), wide)
        fgrad[span, :] = dot(weights, full_t[:, :, span].reshape(4 * SIDE, wide)).T
        return carry

    halves = rows // wide // 2
    lax.fori_loop(0, halves, feature_part, 0)

    for yy in group_y:
        arrived(sum_y, recv_y.at[yy])
    total = got_y[0]
    for yy in range(1, ny):
        total = total + got_y[yy]
    sum_y[...] = total

    stage_z = []
    for zz in group_z:
        stage_z.append(remote(sum_y, got_z.at[z], send_z.at[zz], recv_z.at[z], at(x, zz, y), c))
        stage_z[-1].start()
    got_z[z] = total
    lax.fori_loop(halves, 2 * halves, feature_part, 0)
    for zz in group_z:
        arrived(sum_y, recv_z.at[zz])
    total = got_z[0]
    for zz in range(1, nz):
        total = total + got_z[zz]
    every[x, own_piece, :] = total

    back = []
    for yy in group_y:
        back.append(remote(
            every.at[x, own_piece], every.at[x, own_piece], send_ay.at[yy], recv_ay.at[y], at(x, z, yy), c))
        back[-1].start()
    for yy in [y] + group_y[::-1]:
        rows_of = pl.ds(pl.multiple_of(yy * piece, piece), piece)
        if yy is not y:
            arrived(every.at[x, rows_of], recv_ay.at[yy])
        for xx in group_ax:
            back.append(remote(
                every.at[x, rows_of], every.at[x, rows_of], send_ax.at[xx, yy], recv_ax.at[x, yy], at(xx, z, y), c))
            back[-1].start()
    for yy in [y] + group_y[::-1]:
        rows_of = pl.ds(pl.multiple_of(yy * piece, piece), piece)
        for xx in group_ax:
            arrived(every.at[xx, rows_of], recv_ax.at[xx, yy])
    for which in range(2):
        for cc in range(2):
            base = (2 * cc + which) * share
            value = jnp.concatenate([every[q, base:base + share, :] for q in range(nx)], axis=0)
            wgrad[which, :, cc * SIDE:(cc + 1) * SIDE] = value.T

    for copy in [pair_feat, pair_grad, pair_sum] + sums + stage_x[0] + stage_x[1] + stage_y + stage_z + back:
        copy.wait_send()


def body(torus, features, out_grad, block_tiles, block_cols, self_weight, neighbor_weight):
    nx, nz, ny = torus
    rows, columns = features.shape
    width = self_weight.shape[1]
    count = block_tiles.shape[0]
    share = SIDE // nx
    piece = 4 * share // ny
    dma = pltpu.SemaphoreType.DMA
    feature_grad, weight_grad = pl.pallas_call(
        functools.partial(kernel, torus),
        out_shape=(pltpu.VMEM((rows, columns), F32), pltpu.VMEM((2, columns, width), F32)),
        in_specs=[pl.BlockSpec(memory_space=pl.ANY)] * 6,
        out_specs=(pl.BlockSpec(memory_space=pltpu.VMEM),) * 2,
        scratch_shapes=[
            pltpu.VMEM((count, SIDE, SIDE), BF16),
            pltpu.VMEM((rows, 2 * SIDE), BF16),
            pltpu.VMEM((rows, columns), BF16),
            pltpu.VMEM((2, SIDE, width), BF16),
            pltpu.VMEM((1, count), jnp.int32),
            pltpu.VMEM((8, SIDE), jnp.int32),
            pltpu.SMEM((8, SIDE), jnp.int32),
            pltpu.VMEM((count + 1, SIDE, SIDE), F32),
            pltpu.VMEM((4, SIDE, rows), BF16),
            pltpu.VMEM((SIDE, rows), BF16),
            pltpu.VMEM((2, HALO, SIDE, SIDE), BF16),
            pltpu.VMEM((2, HALO, SIDE, SIDE), BF16),
            pltpu.VMEM((2, 2, nx, share, SIDE), F32),
            pltpu.VMEM((2, 2 * nx, share, SIDE), F32),
            pltpu.VMEM((4 * share, SIDE), F32),
            pltpu.VMEM((ny, piece, SIDE), F32),
            pltpu.VMEM((piece, SIDE), F32),
            pltpu.VMEM((nz, piece, SIDE), F32),
            pltpu.VMEM((nx, 4 * share, SIDE), F32),
            dma((6,)), dma((CHUNKS,)), dma((3,)), dma((3,)), dma((2,)), dma((2,)),
            dma((2, 2 * nx)), dma((2, 2 * nx)), dma((ny,)), dma((ny,)), dma((nz,)), dma((nz,)),
            dma((ny,)), dma((ny,)), dma((nx, ny)), dma((nx, ny)),
        ],
        compiler_params=pltpu.CompilerParams(
            collective_id=0, has_side_effects=True, vmem_limit_bytes=VMEM_BYTES
        ),
        cost_estimate=pl.CostEstimate(flops=1100000000, bytes_accessed=4500000, transcendentals=0),
    )(features, out_grad, block_tiles, block_cols.reshape(1, count), self_weight, neighbor_weight)
    return feature_grad, weight_grad[0], weight_grad[1]


def solution(mesh):
    in_specs = (
        P("blk", "rep"),
        P("blk", "rep"),
        P("blk", None, None),
        P("blk"),
        P("rep", None),
        P("rep", None),
    )
    out_specs = (P("blk", "rep"), P("rep", None), P("rep", None))
    step = functools.partial(body, TORUS)
    return jax.shard_map(step, mesh=mesh, in_specs=in_specs, out_specs=out_specs, check_vma=False)
```

```python
import functools

import jax
import jax.numpy as jnp
from jax import lax
from jax.experimental import pallas as pl
from jax.experimental.pallas import tpu as pltpu
from jax.sharding import PartitionSpec as P

HALO = 2
SIDE = 128
TORUS = (4, 12, 8)
CHUNKS = 4
VMEM_BYTES = 60 * 1024 * 1024
BF16, F32 = jnp.bfloat16, jnp.float32


def dot(a, b):
    return jnp.dot(a, b, preferred_element_type=F32)


def kernel(
    torus,
    feat, grad, tiles, cols, self_w, neigh_w,
    fgrad, wgrad,
    tile_buf, feat_buf, grad_buf, w_buf, cols_v, index_v, index_s,
    chain, full_t, low_t, rim_tiles, rim_out, rim_in,
    part, got_x, sum_x, got_y, sum_y, got_z, every,
    load_sem, tile_sem, pair_send, pair_recv, rim_send, rim_recv,
    heard_1, heard_2, heard_3, send_x, recv_x, send_y, recv_y, send_z, recv_z, send_ay, recv_ay, send_ax, recv_ax,
):
    nx, nz, ny = torus
    n = nx * nz * ny
    m, c = lax.axis_index("blk"), lax.axis_index("rep")
    x, z, y = m // (nz * ny), (m // ny) % nz, m % ny
    rows = grad.shape[0]
    blocks = rows // SIDE
    count = tiles.shape[0]
    per = count // blocks
    up, down = (m + 1) % n, (m + n - 1) % n
    other = 1 - c

    def at(xx, zz, yy):
        return (xx * nz + zz) * ny + yy

    def far_first(size):
        return sorted(range(1, size), key=lambda k: -min(k, size - k))

    group_x = [((x + k) % nx, (c + j) % 2) for k in far_first(nx) + [0] for j in ((0, 1) if k else (1,))]
    group_y = [(y + k) % ny for k in far_first(ny)]
    group_z = [(z + k) % nz for k in far_first(nz)]
    group_ax = [(x + k) % nx for k in far_first(nx)]

    def remote(src, dst, send, recv, blk, rep):
        return pltpu.make_async_remote_copy(
            src_ref=src, dst_ref=dst, send_sem=send, recv_sem=recv,
            device_id={"blk": blk, "rep": rep}, device_id_type=pl.DeviceIdType.MESH,
        )

    def arrived(like, recv):
        pltpu.make_async_copy(like, like, recv).wait()

    def signal(sem, blk, rep):
        pl.semaphore_signal(sem, inc=1, device_id={"blk": blk, "rep": rep}, device_id_type=pl.DeviceIdType.MESH)

    barrier = pltpu.get_barrier_semaphore()
    near = [(at(x, (z + k) % nz, y), c) for k in (1, nz - 1)] + [(at(x, z, (y + k) % ny), c) for k in (1, ny - 1)]
    near += [(at((x + k) % nx, z, y), cc) for k in (1, nx - 1) for cc in (c, other)] + [(m, other), (up, c), (down, c)]
    for blk, rep in near:
        signal(barrier, blk, rep)

    def pass_on(sems, step, axes):
        for k in (step, -step):
            to = {"x": at((x + k + nx) % nx, z, y), "y": at(x, z, (y + k + ny) % ny), "z": at(x, (z + k + nz) % nz, y)}
            for i, axis in enumerate(axes):
                signal(sems.at[i], to[axis], c)

    def hear(sems, axes):
        for i in range(len(axes)):
            pl.semaphore_wait(sems.at[i], 2)

    own_cols = pl.ds(pl.multiple_of(c * SIDE, SIDE), SIDE)
    rim = HALO * SIDE
    ends = [k for k in range(HALO)] + [blocks - HALO + k for k in range(HALO)]
    rim_loads = [
        pltpu.make_async_copy(grad.at[pl.ds(0, rim)], grad_buf.at[pl.ds(0, rim)], load_sem.at[0]),
        pltpu.make_async_copy(grad.at[pl.ds(rows - rim, rim)], grad_buf.at[pl.ds(rows - rim, rim)], load_sem.at[1]),
    ]
    for k, b in enumerate(ends):
        rim_loads.append(pltpu.make_async_copy(tiles.at[b * per], rim_tiles.at[k], load_sem.at[2 + k]))
    load_cols = pltpu.make_async_copy(cols, cols_v, load_sem.at[6])
    load_grad = pltpu.make_async_copy(
        grad.at[pl.ds(rim, rows - 2 * rim)], grad_buf.at[pl.ds(rim, rows - 2 * rim)], load_sem.at[7])
    chunk = count // CHUNKS
    tile_loads = [
        pltpu.make_async_copy(tiles.at[pl.ds(i * chunk, chunk)], tile_buf.at[pl.ds(i * chunk, chunk)], tile_sem.at[i])
        for i in range(CHUNKS)
    ]
    late_loads = [
        pltpu.make_async_copy(feat, feat_buf.at[:, own_cols], load_sem.at[8]),
        pltpu.make_async_copy(self_w, w_buf.at[0], load_sem.at[9]),
        pltpu.make_async_copy(neigh_w, w_buf.at[1], load_sem.at[10]),
    ]
    for copy in [load_cols] + rim_loads + [load_grad] + tile_loads + late_loads:
        copy.start()

    load_cols.wait()
    slot = cols_v[...] - m * blocks
    slot = jnp.concatenate([slot, jnp.full((1, SIDE - count), -1, jnp.int32)], axis=1)
    across = jnp.broadcast_to(slot, (SIDE, SIDE))
    along = across.T
    row = lax.broadcasted_iota(jnp.int32, (SIDE, SIDE), 0)
    lane = lax.broadcasted_iota(jnp.int32, (SIDE, SIDE), 1)
    before = jnp.max(jnp.where((across == along) & (row < lane), row, -1), axis=0, keepdims=True)
    final = jnp.max(jnp.where((along == lane) & (row < count), row, -1), axis=0, keepdims=True)
    index_v[0:1, :] = jnp.where(before < 0, count, before)
    index_v[1:2, :] = jnp.where(final < 0, count, final)
    to_scalar = pltpu.make_async_copy(index_v, index_s, load_sem.at[11])
    to_scalar.start()
    chain[count] = jnp.zeros((SIDE, SIDE), F32)

    for copy in rim_loads:
        copy.wait()
    for k, b in enumerate(ends):
        rim_out[k // HALO, k % HALO] = dot(grad_buf[b * SIDE:(b + 1) * SIDE, :].T, rim_tiles[k]).astype(BF16)

    pl.semaphore_wait(barrier, len(near))
    sums = [
        remote(rim_out.at[0], rim_in.at[0], rim_send.at[0], rim_recv.at[0], down, c),
        remote(rim_out.at[1], rim_in.at[1], rim_send.at[1], rim_recv.at[1], up, c),
    ]
    for copy in sums:
        copy.start()
    pair_feat = remote(feat, feat_buf.at[:, own_cols], pair_send.at[0], pair_recv.at[0], m, other)
    pair_feat.start()
    pass_on(heard_1, 1, "xyz")
    to_scalar.wait()
    load_grad.wait()

    for b in range(blocks):
        span = pl.ds(b * SIDE, SIDE)
        full_t[c, :, span] = grad_buf[span, :].T

    def tile_work(i):
        tile_loads[i].wait()
        for b in range(i * blocks // CHUNKS, (i + 1) * blocks // CHUNKS):
            product = dot(
                full_t[c, :, pl.ds(b * SIDE, SIDE)],
                jnp.concatenate([tile_buf[b * per + k] for k in range(per)], axis=1))
            for k in range(per):
                t = b * per + k
                chain[t] = chain[index_s[0, t]] + product[:, k * SIDE:(k + 1) * SIDE]

    for i in range(CHUNKS // 2):
        tile_work(i)

    share = SIDE // nx
    stage_x = [[], []]

    def send_share(which, value):
        for r in range(2):
            for q in range(nx):
                part[which, r, q] = value[q * share:(q + 1) * share, r * SIDE:(r + 1) * SIDE]
        for xx, cc in group_x:
            stage_x[which].append(remote(
                part.at[which, cc, xx], got_x.at[which, 2 * x + c],
                send_x.at[which, 2 * xx + cc], recv_x.at[which, 2 * x + c], at(xx, z, y), cc))
            stage_x[which][-1].start()
        got_x[which, 2 * x + c] = part[which, c, x]

    late_loads[0].wait()
    pair_feat.wait_recv()
    hear(heard_1, "xyz")
    pass_on(heard_2, 2, "yz")
    send_share(0, dot(full_t[c], feat_buf[...]))
    for i in range(CHUNKS // 2, CHUNKS):
        tile_work(i)

    def column_block(b, value):
        span = pl.ds(b * SIDE, SIDE)
        hi = value.astype(BF16)
        full_t[2 + c, :, span] = hi
        low_t[:, span] = (value - hi.astype(F32)).astype(BF16)

    for b in range(HALO, blocks - HALO):
        column_block(b, chain[index_s[1, b]])

    def product(low, high):
        span = pl.ds(low, high - low)
        return dot(full_t[2 + c, :, span], feat_buf[span, :]) + dot(low_t[:, span], feat_buf[span, :])

    inner = product(rim, rows - rim)
    for copy in sums:
        copy.wait_recv()
    for k in range(HALO):
        b = blocks - 1 - k
        column_block(b, chain[index_s[1, b]] + rim_in[0, k].astype(F32))
        b = HALO - 1 - k
        column_block(b, chain[index_s[1, b]] + rim_in[1, k].astype(F32))
    send_share(1, inner + product(0, rim) + product(rows - rim, rows))
    pair_grad = remote(full_t.at[c], full_t.at[c], pair_send.at[1], pair_recv.at[1], m, other)
    pair_grad.start()
    pair_sum = remote(full_t.at[2 + c], full_t.at[2 + c], pair_send.at[2], pair_recv.at[2], m, other)
    pair_sum.start()
    hear(heard_2, "yz")
    pass_on(heard_3, 2, "z")
    for copy in late_loads[1:]:
        copy.wait()

    for which in range(2):
        for xx, cc in group_x:
            arrived(part.at[which, c, x], recv_x.at[which, 2 * xx + cc])
        for cc in range(2):
            total = got_x[which, cc]
            for xx in range(1, nx):
                total = total + got_x[which, 2 * xx + cc]
            sum_x[(2 * cc + which) * share:(2 * cc + which + 1) * share, :] = total

    piece = 4 * share // ny
    own_piece = pl.ds(pl.multiple_of(y * piece, piece), piece)
    stage_y = []
    for yy in group_y:
        stage_y.append(remote(
            sum_x.at[pl.ds(pl.multiple_of(yy * piece, piece), piece)], got_y.at[y],
            send_y.at[yy], recv_y.at[y], at(x, z, yy), c))
        stage_y[-1].start()
    got_y[y] = sum_x[own_piece, :]

    pair_grad.wait_recv()
    pair_sum.wait_recv()
    weights = jnp.concatenate([w_buf[0], w_buf[1]], axis=1)
    wide = 2 * SIDE

    def feature_part(low, high):
        for i in range(low, high):
            span = pl.ds(i * wide, wide)
            fgrad[span, :] = dot(weights, full_t[:, :, span].reshape(4 * SIDE, wide)).T

    halves = rows // wide // 2
    feature_part(0, halves)

    for yy in group_y:
        arrived(sum_y, recv_y.at[yy])
    total = got_y[0]
    for yy in range(1, ny):
        total = total + got_y[yy]
    sum_y[...] = total

    hear(heard_3, "z")
    stage_z = []
    for zz in group_z:
        stage_z.append(remote(sum_y, got_z.at[z], send_z.at[zz], recv_z.at[z], at(x, zz, y), c))
        stage_z[-1].start()
    got_z[z] = total
    feature_part(halves, 2 * halves)
    for copy in [pair_feat, pair_grad, pair_sum] + sums + stage_x[0] + stage_x[1] + stage_y:
        copy.wait_send()
    for zz in group_z:
        arrived(sum_y, recv_z.at[zz])
    total = got_z[0]
    for zz in range(1, nz):
        total = total + got_z[zz]
    every[x, own_piece, :] = total

    back = []
    for yy in group_y:
        back.append(remote(
            every.at[x, own_piece], every.at[x, own_piece], send_ay.at[yy], recv_ay.at[y], at(x, z, yy), c))
        back[-1].start()
    for yy in [y] + group_y[::-1]:
        rows_of = pl.ds(pl.multiple_of(yy * piece, piece), piece)
        if yy is not y:
            arrived(every.at[x, rows_of], recv_ay.at[yy])
        for xx in group_ax:
            back.append(remote(
                every.at[x, rows_of], every.at[x, rows_of], send_ax.at[xx, yy], recv_ax.at[x, yy], at(xx, z, y), c))
            back[-1].start()
    for copy in stage_z + back[:ny + nx - 2]:
        copy.wait_send()
    for yy in [y] + group_y[::-1]:
        rows_of = pl.ds(pl.multiple_of(yy * piece, piece), piece)
        for xx in group_ax:
            arrived(every.at[xx, rows_of], recv_ax.at[xx, yy])
    for which in range(2):
        for cc in range(2):
            base = (2 * cc + which) * share
            value = jnp.concatenate([every[q, base:base + share, :] for q in range(nx)], axis=0)
            wgrad[which, :, cc * SIDE:(cc + 1) * SIDE] = value.T

    for copy in back[ny + nx - 2:]:
        copy.wait_send()


def body(torus, features, out_grad, block_tiles, block_cols, self_weight, neighbor_weight):
    nx, nz, ny = torus
    rows, columns = features.shape
    width = self_weight.shape[1]
    count = block_tiles.shape[0]
    share = SIDE // nx
    piece = 4 * share // ny
    dma = pltpu.SemaphoreType.DMA
    anywhere = pl.BlockSpec(memory_space=pl.ANY)
    heard = pltpu.SemaphoreType.REGULAR((3,))
    feature_grad, weight_grad = pl.pallas_call(
        functools.partial(kernel, torus),
        out_shape=(pltpu.VMEM((rows, columns), F32), pltpu.VMEM((2, columns, width), F32)),
        in_specs=[anywhere] * 6,
        out_specs=(pl.BlockSpec(memory_space=pltpu.VMEM),) * 2,
        scratch_shapes=[
            pltpu.VMEM((count, SIDE, SIDE), BF16),
            pltpu.VMEM((rows, 2 * SIDE), BF16),
            pltpu.VMEM((rows, columns), BF16),
            pltpu.VMEM((2, SIDE, width), BF16),
            pltpu.VMEM((1, count), jnp.int32),
            pltpu.VMEM((8, SIDE), jnp.int32),
            pltpu.SMEM((8, SIDE), jnp.int32),
            pltpu.VMEM((count + 1, SIDE, SIDE), F32),
            pltpu.VMEM((4, SIDE, rows), BF16),
            pltpu.VMEM((SIDE, rows), BF16),
            pltpu.VMEM((2 * HALO, SIDE, SIDE), BF16),
            pltpu.VMEM((2, HALO, SIDE, SIDE), BF16),
            pltpu.VMEM((2, HALO, SIDE, SIDE), BF16),
            pltpu.VMEM((2, 2, nx, share, SIDE), F32),
            pltpu.VMEM((2, 2 * nx, share, SIDE), F32),
            pltpu.VMEM((4 * share, SIDE), F32),
            pltpu.VMEM((ny, piece, SIDE), F32),
            pltpu.VMEM((piece, SIDE), F32),
            pltpu.VMEM((nz, piece, SIDE), F32),
            pltpu.VMEM((nx, 4 * share, SIDE), F32),
            dma((12,)), dma((CHUNKS,)), dma((3,)), dma((3,)), dma((2,)), dma((2,)),
            heard, heard, heard,
            dma((2, 2 * nx)), dma((2, 2 * nx)), dma((ny,)), dma((ny,)), dma((nz,)), dma((nz,)),
            dma((ny,)), dma((ny,)), dma((nx, ny)), dma((nx, ny)),
        ],
        compiler_params=pltpu.CompilerParams(
            collective_id=0, has_side_effects=True, vmem_limit_bytes=VMEM_BYTES
        ),
        cost_estimate=pl.CostEstimate(flops=1100000000, bytes_accessed=4500000, transcendentals=0),
    )(features, out_grad, block_tiles, block_cols.reshape(1, count), self_weight, neighbor_weight)
    return feature_grad, weight_grad[0], weight_grad[1]


def solution(mesh):
    in_specs = (
        P("blk", "rep"),
        P("blk", "rep"),
        P("blk", None, None),
        P("blk"),
        P("rep", None),
        P("rep", None),
    )
    out_specs = (P("blk", "rep"), P("rep", None), P("rep", None))
    step = functools.partial(body, TORUS)
    return jax.shard_map(step, mesh=mesh, in_specs=in_specs, out_specs=out_specs, check_vma=False)
```

```python
import functools

import jax
import jax.numpy as jnp
from jax import lax
from jax.experimental import pallas as pl
from jax.experimental.pallas import tpu as pltpu
from jax.sharding import PartitionSpec as P

HALO = 2
SIDE = 128
TORUS = (4, 12, 8)
CHUNKS = 4
VMEM_BYTES = 60 * 1024 * 1024
BF16, F32 = jnp.bfloat16, jnp.float32


def dot(a, b):
    return jnp.dot(a, b, preferred_element_type=F32)


def kernel(
    torus,
    feat, grad, tiles, cols, self_w, neigh_w,
    fgrad, wgrad,
    tile_buf, feat_buf, grad_buf, w_buf, cols_v, index_v, index_s,
    chain, full_t, low_t, rim_tiles, rim_out, rim_in,
    part, got_x, sum_x, got_y, sum_y, got_z, every,
    load_sem, tile_sem, pair_send, pair_recv, rim_send, rim_recv,
    heard_1, heard_2, heard_3, send_x, recv_x, send_y, recv_y, send_z, recv_z, send_back, recv_back,
):
    nx, nz, ny = torus
    n = nx * nz * ny
    m, c = lax.axis_index("blk"), lax.axis_index("rep")
    x, z, y = m // (nz * ny), (m // ny) % nz, m % ny
    rows = grad.shape[0]
    blocks = rows // SIDE
    count = tiles.shape[0]
    per = count // blocks
    up, down = (m + 1) % n, (m + n - 1) % n
    other = 1 - c

    def at(xx, zz, yy):
        return (xx * nz + zz) * ny + yy

    def far_first(size):
        return sorted(range(1, size), key=lambda k: -min(k, size - k))

    group_x = [((x + k) % nx, (c + j) % 2) for k in far_first(nx) + [0] for j in ((0, 1) if k else (1,))]
    group_y = [(y + k) % ny for k in far_first(ny)]
    group_z = [(z + k) % nz for k in far_first(nz)]

    def remote(src, dst, send, recv, blk, rep):
        return pltpu.make_async_remote_copy(
            src_ref=src, dst_ref=dst, send_sem=send, recv_sem=recv,
            device_id={"blk": blk, "rep": rep}, device_id_type=pl.DeviceIdType.MESH,
        )

    def arrived(like, recv):
        pltpu.make_async_copy(like, like, recv).wait()

    def signal(sem, blk, rep):
        pl.semaphore_signal(sem, inc=1, device_id={"blk": blk, "rep": rep}, device_id_type=pl.DeviceIdType.MESH)

    barrier = pltpu.get_barrier_semaphore()
    near = [(at(x, (z + k) % nz, y), c) for k in (1, nz - 1)] + [(at(x, z, (y + k) % ny), c) for k in (1, ny - 1)]
    near += [(at((x + k) % nx, z, y), cc) for k in (1, nx - 1) for cc in (c, other)] + [(m, other), (up, c), (down, c)]
    for blk, rep in near:
        signal(barrier, blk, rep)

    def pass_on(sems, step, axes):
        for k in (step, -step):
            to = {"x": at((x + k + nx) % nx, z, y), "y": at(x, z, (y + k + ny) % ny), "z": at(x, (z + k + nz) % nz, y)}
            for i, axis in enumerate(axes):
                signal(sems.at[i], to[axis], c)

    def hear(sems, axes):
        for i in range(len(axes)):
            pl.semaphore_wait(sems.at[i], 2)

    own_cols = pl.ds(pl.multiple_of(c * SIDE, SIDE), SIDE)
    rim = HALO * SIDE
    ends = [k for k in range(HALO)] + [blocks - HALO + k for k in range(HALO)]
    rim_loads = [
        pltpu.make_async_copy(grad.at[pl.ds(0, rim)], grad_buf.at[pl.ds(0, rim)], load_sem.at[0]),
        pltpu.make_async_copy(grad.at[pl.ds(rows - rim, rim)], grad_buf.at[pl.ds(rows - rim, rim)], load_sem.at[1]),
    ]
    for k, b in enumerate(ends):
        rim_loads.append(pltpu.make_async_copy(tiles.at[b * per], rim_tiles.at[k], load_sem.at[2 + k]))
    load_cols = pltpu.make_async_copy(cols, cols_v, load_sem.at[6])
    load_grad = pltpu.make_async_copy(
        grad.at[pl.ds(rim, rows - 2 * rim)], grad_buf.at[pl.ds(rim, rows - 2 * rim)], load_sem.at[7])
    chunk = count // CHUNKS
    tile_loads = [
        pltpu.make_async_copy(tiles.at[pl.ds(i * chunk, chunk)], tile_buf.at[pl.ds(i * chunk, chunk)], tile_sem.at[i])
        for i in range(CHUNKS)
    ]
    late_loads = [
        pltpu.make_async_copy(feat, feat_buf.at[:, own_cols], load_sem.at[8]),
        pltpu.make_async_copy(self_w, w_buf.at[0], load_sem.at[9]),
        pltpu.make_async_copy(neigh_w, w_buf.at[1], load_sem.at[10]),
    ]
    for copy in [load_cols] + rim_loads + [load_grad] + tile_loads + late_loads:
        copy.start()

    load_cols.wait()
    slot = cols_v[...] - m * blocks
    slot = jnp.concatenate([slot, jnp.full((1, SIDE - count), -1, jnp.int32)], axis=1)
    across = jnp.broadcast_to(slot, (SIDE, SIDE))
    along = across.T
    row = lax.broadcasted_iota(jnp.int32, (SIDE, SIDE), 0)
    lane = lax.broadcasted_iota(jnp.int32, (SIDE, SIDE), 1)
    before = jnp.max(jnp.where((across == along) & (row < lane), row, -1), axis=0, keepdims=True)
    final = jnp.max(jnp.where((along == lane) & (row < count), row, -1), axis=0, keepdims=True)
    index_v[0:1, :] = jnp.where(before < 0, count, before)
    index_v[1:2, :] = jnp.where(final < 0, count, final)
    to_scalar = pltpu.make_async_copy(index_v, index_s, load_sem.at[11])
    to_scalar.start()
    chain[count] = jnp.zeros((SIDE, SIDE), F32)

    for copy in rim_loads:
        copy.wait()
    for k, b in enumerate(ends):
        rim_out[k // HALO, k % HALO] = dot(grad_buf[b * SIDE:(b + 1) * SIDE, :].T, rim_tiles[k]).astype(BF16)

    pl.semaphore_wait(barrier, len(near))
    sums = [
        remote(rim_out.at[0], rim_in.at[0], rim_send.at[0], rim_recv.at[0], down, c),
        remote(rim_out.at[1], rim_in.at[1], rim_send.at[1], rim_recv.at[1], up, c),
    ]
    for copy in sums:
        copy.start()
    pair_feat = remote(feat, feat_buf.at[:, own_cols], pair_send.at[0], pair_recv.at[0], m, other)
    pair_feat.start()
    pass_on(heard_1, 1, "xyz")
    to_scalar.wait()
    load_grad.wait()

    for b in range(blocks):
        span = pl.ds(b * SIDE, SIDE)
        full_t[c, :, span] = grad_buf[span, :].T

    def tile_work(i):
        tile_loads[i].wait()
        for b in range(i * blocks // CHUNKS, (i + 1) * blocks // CHUNKS):
            product = dot(
                full_t[c, :, pl.ds(b * SIDE, SIDE)],
                jnp.concatenate([tile_buf[b * per + k] for k in range(per)], axis=1))
            for k in range(per):
                t = b * per + k
                chain[t] = chain[index_s[0, t]] + product[:, k * SIDE:(k + 1) * SIDE]

    for i in range(CHUNKS // 2):
        tile_work(i)

    share = SIDE // nx
    stage_x = [[], []]

    def send_share(which, value):
        for r in range(2):
            for q in range(nx):
                part[which, r, q] = value[q * share:(q + 1) * share, r * SIDE:(r + 1) * SIDE]
        for xx, cc in group_x:
            stage_x[which].append(remote(
                part.at[which, cc, xx], got_x.at[which, 2 * x + c],
                send_x.at[which, 2 * xx + cc], recv_x.at[which, 2 * x + c], at(xx, z, y), cc))
            stage_x[which][-1].start()
        got_x[which, 2 * x + c] = part[which, c, x]

    late_loads[0].wait()
    pair_feat.wait_recv()
    hear(heard_1, "xyz")
    pass_on(heard_2, 2, "yz")
    send_share(0, dot(full_t[c], feat_buf[...]))
    for i in range(CHUNKS // 2, CHUNKS):
        tile_work(i)

    def column_block(b, value):
        span = pl.ds(b * SIDE, SIDE)
        hi = value.astype(BF16)
        full_t[2 + c, :, span] = hi
        low_t[:, span] = (value - hi.astype(F32)).astype(BF16)

    for b in range(HALO, blocks - HALO):
        column_block(b, chain[index_s[1, b]])

    def product(low, high):
        span = pl.ds(low, high - low)
        return dot(full_t[2 + c, :, span], feat_buf[span, :]) + dot(low_t[:, span], feat_buf[span, :])

    inner = product(rim, rows - rim)
    for copy in sums:
        copy.wait_recv()
    for k in range(HALO):
        b = blocks - 1 - k
        column_block(b, chain[index_s[1, b]] + rim_in[0, k].astype(F32))
        b = HALO - 1 - k
        column_block(b, chain[index_s[1, b]] + rim_in[1, k].astype(F32))
    send_share(1, inner + product(0, rim) + product(rows - rim, rows))
    pair_grad = remote(full_t.at[c], full_t.at[c], pair_send.at[1], pair_recv.at[1], m, other)
    pair_grad.start()
    pair_sum = remote(full_t.at[2 + c], full_t.at[2 + c], pair_send.at[2], pair_recv.at[2], m, other)
    pair_sum.start()
    hear(heard_2, "yz")
    pass_on(heard_3, 2, "z")
    for copy in late_loads[1:]:
        copy.wait()

    for which in range(2):
        for xx, cc in group_x:
            arrived(part.at[which, c, x], recv_x.at[which, 2 * xx + cc])
        for cc in range(2):
            total = got_x[which, cc]
            for xx in range(1, nx):
                total = total + got_x[which, 2 * xx + cc]
            sum_x[(2 * cc + which) * share:(2 * cc + which + 1) * share, :] = total

    piece = 4 * share // ny
    own_piece = pl.ds(pl.multiple_of(y * piece, piece), piece)
    stage_y = []
    for yy in group_y:
        stage_y.append(remote(
            sum_x.at[pl.ds(pl.multiple_of(yy * piece, piece), piece)], got_y.at[y],
            send_y.at[yy], recv_y.at[y], at(x, z, yy), c))
        stage_y[-1].start()
    got_y[y] = sum_x[own_piece, :]

    pair_grad.wait_recv()
    pair_sum.wait_recv()
    weights = jnp.concatenate([w_buf[0], w_buf[1]], axis=1)
    wide = 2 * SIDE

    def feature_part(low, high):
        for i in range(low, high):
            span = pl.ds(i * wide, wide)
            fgrad[span, :] = dot(weights, full_t[:, :, span].reshape(4 * SIDE, wide)).T

    halves = rows // wide // 2
    feature_part(0, halves)

    for yy in group_y:
        arrived(sum_y, recv_y.at[yy])
    total = got_y[0]
    for yy in range(1, ny):
        total = total + got_y[yy]
    sum_y[...] = total

    hear(heard_3, "z")
    stage_z = []
    for zz in group_z:
        stage_z.append(remote(sum_y, got_z.at[z], send_z.at[zz], recv_z.at[z], at(x, zz, y), c))
        stage_z[-1].start()
    got_z[z] = total
    feature_part(halves, 2 * halves)
    for copy in [pair_feat, pair_grad, pair_sum] + sums + stage_x[0] + stage_x[1] + stage_y:
        copy.wait_send()
    for zz in group_z:
        arrived(sum_y, recv_z.at[zz])
    total = got_z[0]
    for zz in range(1, nz):
        total = total + got_z[zz]
    every[x, own_piece, :] = total.astype(BF16)

    plane = [(i, j) for i in range(nx) for j in range(ny) if i or j]
    plane = [((x + i) % nx, (y + j) % ny) for i, j in sorted(plane, key=lambda p: -min(p[0], nx - p[0]) - min(p[1], ny - p[1]))]
    back = []
    for xx, yy in plane:
        back.append(remote(
            every.at[x, own_piece], every.at[x, own_piece], send_back.at[xx, yy], recv_back.at[x, y], at(xx, z, yy), c))
        back[-1].start()
    for copy in stage_z:
        copy.wait_send()
    for xx, yy in plane[::-1]:
        arrived(every.at[xx, pl.ds(pl.multiple_of(yy * piece, piece), piece)], recv_back.at[xx, yy])
    for which in range(2):
        for cc in range(2):
            base = (2 * cc + which) * share
            value = jnp.concatenate([every[q, base:base + share, :] for q in range(nx)], axis=0)
            wgrad[which, :, cc * SIDE:(cc + 1) * SIDE] = value.astype(F32).T

    for copy in back:
        copy.wait_send()


def body(torus, features, out_grad, block_tiles, block_cols, self_weight, neighbor_weight):
    nx, nz, ny = torus
    rows, columns = features.shape
    width = self_weight.shape[1]
    count = block_tiles.shape[0]
    share = SIDE // nx
    piece = 4 * share // ny
    dma = pltpu.SemaphoreType.DMA
    anywhere = pl.BlockSpec(memory_space=pl.ANY)
    heard = pltpu.SemaphoreType.REGULAR((3,))
    feature_grad, weight_grad = pl.pallas_call(
        functools.partial(kernel, torus),
        out_shape=(pltpu.VMEM((rows, columns), F32), pltpu.VMEM((2, columns, width), F32)),
        in_specs=[anywhere] * 6,
        out_specs=(pl.BlockSpec(memory_space=pltpu.VMEM),) * 2,
        scratch_shapes=[
            pltpu.VMEM((count, SIDE, SIDE), BF16),
            pltpu.VMEM((rows, 2 * SIDE), BF16),
            pltpu.VMEM((rows, columns), BF16),
            pltpu.VMEM((2, SIDE, width), BF16),
            pltpu.VMEM((1, count), jnp.int32),
            pltpu.VMEM((8, SIDE), jnp.int32),
            pltpu.SMEM((8, SIDE), jnp.int32),
            pltpu.VMEM((count + 1, SIDE, SIDE), F32),
            pltpu.VMEM((4, SIDE, rows), BF16),
            pltpu.VMEM((SIDE, rows), BF16),
            pltpu.VMEM((2 * HALO, SIDE, SIDE), BF16),
            pltpu.VMEM((2, HALO, SIDE, SIDE), BF16),
            pltpu.VMEM((2, HALO, SIDE, SIDE), BF16),
            pltpu.VMEM((2, 2, nx, share, SIDE), F32),
            pltpu.VMEM((2, 2 * nx, share, SIDE), F32),
            pltpu.VMEM((4 * share, SIDE), F32),
            pltpu.VMEM((ny, piece, SIDE), F32),
            pltpu.VMEM((piece, SIDE), F32),
            pltpu.VMEM((nz, piece, SIDE), F32),
            pltpu.VMEM((nx, 4 * share, SIDE), BF16),
            dma((12,)), dma((CHUNKS,)), dma((3,)), dma((3,)), dma((2,)), dma((2,)),
            heard, heard, heard,
            dma((2, 2 * nx)), dma((2, 2 * nx)), dma((ny,)), dma((ny,)), dma((nz,)), dma((nz,)),
            dma((nx, ny)), dma((nx, ny)),
        ],
        compiler_params=pltpu.CompilerParams(
            collective_id=0, has_side_effects=True, vmem_limit_bytes=VMEM_BYTES
        ),
        cost_estimate=pl.CostEstimate(flops=1100000000, bytes_accessed=4500000, transcendentals=0),
    )(features, out_grad, block_tiles, block_cols.reshape(1, count), self_weight, neighbor_weight)
    return feature_grad, weight_grad[0], weight_grad[1]


def solution(mesh):
    in_specs = (
        P("blk", "rep"),
        P("blk", "rep"),
        P("blk", None, None),
        P("blk"),
        P("rep", None),
        P("rep", None),
    )
    out_specs = (P("blk", "rep"), P("rep", None), P("rep", None))
    step = functools.partial(body, TORUS)
    return jax.shard_map(step, mesh=mesh, in_specs=in_specs, out_specs=out_specs, check_vma=False)
```

```python
import functools

import jax
import jax.numpy as jnp
from jax import lax
from jax.experimental import pallas as pl
from jax.experimental.pallas import tpu as pltpu
from jax.sharding import PartitionSpec as P

HALO = 2
SIDE = 128
TORUS = (4, 12, 8)
CHUNKS = 4
VMEM_BYTES = 60 * 1024 * 1024
BF16, F32 = jnp.bfloat16, jnp.float32


def dot(a, b):
    return jnp.dot(a, b, preferred_element_type=F32)


def kernel(
    torus,
    feat, grad, tiles, cols, self_w, neigh_w,
    fgrad, wgrad,
    tile_buf, feat_buf, grad_buf, w_buf, cols_v, index_v, index_s,
    chain, full_t, low_t, rim_tiles, rim_out, rim_in,
    part, got_x, sum_x, got_y, sum_y, got_z, every,
    load_sem, tile_sem, pair_send, pair_recv, rim_send, rim_recv,
    heard_1, heard_2, heard_3, send_x, recv_x, send_y, recv_y, send_z, recv_z, send_back, recv_back,
):
    nx, nz, ny = torus
    n = nx * nz * ny
    m, c = lax.axis_index("blk"), lax.axis_index("rep")
    x, z, y = m // (nz * ny), (m // ny) % nz, m % ny
    rows = grad.shape[0]
    blocks = rows // SIDE
    count = tiles.shape[0]
    per = count // blocks
    up, down = (m + 1) % n, (m + n - 1) % n
    other = 1 - c

    def at(xx, zz, yy):
        return (xx * nz + zz) * ny + yy

    def far_first(size):
        return sorted(range(1, size), key=lambda k: -min(k, size - k))

    group_x = [((x + k) % nx, (c + j) % 2) for k in far_first(nx) + [0] for j in ((0, 1) if k else (1,))]
    group_y = [(y + k) % ny for k in far_first(ny)]
    group_z = [(z + k) % nz for k in far_first(nz)]

    def remote(src, dst, send, recv, blk, rep):
        return pltpu.make_async_remote_copy(
            src_ref=src, dst_ref=dst, send_sem=send, recv_sem=recv,
            device_id={"blk": blk, "rep": rep}, device_id_type=pl.DeviceIdType.MESH,
        )

    def arrived(like, recv):
        pltpu.make_async_copy(like, like, recv).wait()

    def signal(sem, blk, rep):
        pl.semaphore_signal(sem, inc=1, device_id={"blk": blk, "rep": rep}, device_id_type=pl.DeviceIdType.MESH)

    barrier = pltpu.get_barrier_semaphore()
    near = [(up, c), (down, c)]
    near += [(at(x, (z + k) % nz, y), c) for k in (1, nz - 1)] + [(at(x, z, (y + k) % ny), c) for k in (1, ny - 1)]
    near += [(at((x + k) % nx, z, y), cc) for k in (1, nx - 1) for cc in (c, other)] + [(m, other)]
    for blk, rep in near:
        signal(barrier, blk, rep)

    def pass_on(sems, step, axes):
        for k in (step, -step):
            to = {"x": at((x + k + nx) % nx, z, y), "y": at(x, z, (y + k + ny) % ny), "z": at(x, (z + k + nz) % nz, y)}
            for i, axis in enumerate(axes):
                signal(sems.at[i], to[axis], c)

    def hear(sems, axes):
        for i in range(len(axes)):
            pl.semaphore_wait(sems.at[i], 2)

    own_cols = pl.ds(pl.multiple_of(c * SIDE, SIDE), SIDE)
    rim = HALO * SIDE
    ends = [k for k in range(HALO)] + [blocks - HALO + k for k in range(HALO)]
    rim_loads = [
        pltpu.make_async_copy(grad.at[pl.ds(0, rim)], grad_buf.at[pl.ds(0, rim)], load_sem.at[0]),
        pltpu.make_async_copy(grad.at[pl.ds(rows - rim, rim)], grad_buf.at[pl.ds(rows - rim, rim)], load_sem.at[1]),
    ]
    for k, b in enumerate(ends):
        rim_loads.append(pltpu.make_async_copy(tiles.at[b * per], rim_tiles.at[k], load_sem.at[2 + k]))
    load_cols = pltpu.make_async_copy(cols, cols_v, load_sem.at[6])
    load_grad = pltpu.make_async_copy(
        grad.at[pl.ds(rim, rows - 2 * rim)], grad_buf.at[pl.ds(rim, rows - 2 * rim)], load_sem.at[7])
    chunk = count // CHUNKS
    tile_loads = [
        pltpu.make_async_copy(tiles.at[pl.ds(i * chunk, chunk)], tile_buf.at[pl.ds(i * chunk, chunk)], tile_sem.at[i])
        for i in range(CHUNKS)
    ]
    late_loads = [
        pltpu.make_async_copy(feat, feat_buf.at[:, own_cols], load_sem.at[8]),
        pltpu.make_async_copy(self_w, w_buf.at[0], load_sem.at[9]),
        pltpu.make_async_copy(neigh_w, w_buf.at[1], load_sem.at[10]),
    ]
    for copy in [load_cols] + rim_loads + [load_grad] + tile_loads + late_loads:
        copy.start()

    load_cols.wait()
    slot = cols_v[...] - m * blocks
    slot = jnp.concatenate([slot, jnp.full((1, SIDE - count), -1, jnp.int32)], axis=1)
    across = jnp.broadcast_to(slot, (SIDE, SIDE))
    along = across.T
    row = lax.broadcasted_iota(jnp.int32, (SIDE, SIDE), 0)
    lane = lax.broadcasted_iota(jnp.int32, (SIDE, SIDE), 1)
    before = jnp.max(jnp.where((across == along) & (row < lane), row, -1), axis=0, keepdims=True)
    final = jnp.max(jnp.where((along == lane) & (row < count), row, -1), axis=0, keepdims=True)
    index_v[0:1, :] = jnp.where(before < 0, count, before)
    index_v[1:2, :] = jnp.where(final < 0, count, final)
    to_scalar = pltpu.make_async_copy(index_v, index_s, load_sem.at[11])
    to_scalar.start()
    chain[count] = jnp.zeros((SIDE, SIDE), F32)

    for copy in rim_loads:
        copy.wait()
    for k, b in enumerate(ends):
        rim_out[k // HALO, k % HALO] = dot(grad_buf[b * SIDE:(b + 1) * SIDE, :].T, rim_tiles[k]).astype(BF16)

    pl.semaphore_wait(barrier, len(near))
    sums = [
        remote(rim_out.at[0], rim_in.at[0], rim_send.at[0], rim_recv.at[0], down, c),
        remote(rim_out.at[1], rim_in.at[1], rim_send.at[1], rim_recv.at[1], up, c),
    ]
    for copy in sums:
        copy.start()
    pair_feat = remote(feat, feat_buf.at[:, own_cols], pair_send.at[0], pair_recv.at[0], m, other)
    pair_feat.start()
    pass_on(heard_1, 1, "xyz")
    to_scalar.wait()
    load_grad.wait()

    for b in range(blocks):
        span = pl.ds(b * SIDE, SIDE)
        full_t[c, :, span] = grad_buf[span, :].T

    def tile_work(i):
        tile_loads[i].wait()
        for b in range(i * blocks // CHUNKS, (i + 1) * blocks // CHUNKS):
            product = dot(
                full_t[c, :, pl.ds(b * SIDE, SIDE)],
                jnp.concatenate([tile_buf[b * per + k] for k in range(per)], axis=1))
            for k in range(per):
                t = b * per + k
                chain[t] = chain[index_s[0, t]] + product[:, k * SIDE:(k + 1) * SIDE]

    for i in range(CHUNKS // 2):
        tile_work(i)

    share = SIDE // nx
    stage_x = [[], []]

    def send_share(which, value):
        for r in range(2):
            for q in range(nx):
                part[which, r, q] = value[q * share:(q + 1) * share, r * SIDE:(r + 1) * SIDE]
        for xx, cc in group_x:
            stage_x[which].append(remote(
                part.at[which, cc, xx], got_x.at[which, 2 * x + c],
                send_x.at[which, 2 * xx + cc], recv_x.at[which, 2 * x + c], at(xx, z, y), cc))
            stage_x[which][-1].start()
        got_x[which, 2 * x + c] = part[which, c, x]

    late_loads[0].wait()
    pair_feat.wait_recv()
    hear(heard_1, "xyz")
    pass_on(heard_2, 2, "yz")
    send_share(0, dot(full_t[c], feat_buf[...]))
    for i in range(CHUNKS // 2, CHUNKS):
        tile_work(i)

    def column_block(b, value):
        span = pl.ds(b * SIDE, SIDE)
        hi = value.astype(BF16)
        full_t[2 + c, :, span] = hi
        low_t[:, span] = (value - hi.astype(F32)).astype(BF16)

    for b in range(HALO, blocks - HALO):
        column_block(b, chain[index_s[1, b]])

    def product(*spans):
        spans = [pl.ds(low, high - low) for low, high in spans]
        right = jnp.concatenate([feat_buf[span, :] for span in spans], axis=0)
        high_part = jnp.concatenate([full_t[2 + c, :, span] for span in spans], axis=1)
        low_part = jnp.concatenate([low_t[:, span] for span in spans], axis=1)
        return dot(high_part, right) + dot(low_part, right)

    inner = product((rim, rows - rim))
    for copy in sums:
        copy.wait_recv()
    for k in range(HALO):
        b = blocks - 1 - k
        column_block(b, chain[index_s[1, b]] + rim_in[0, k].astype(F32))
        b = HALO - 1 - k
        column_block(b, chain[index_s[1, b]] + rim_in[1, k].astype(F32))
    send_share(1, inner + product((0, rim), (rows - rim, rows)))
    pair_grad = remote(full_t.at[c], full_t.at[c], pair_send.at[1], pair_recv.at[1], m, other)
    pair_grad.start()
    pair_sum = remote(full_t.at[2 + c], full_t.at[2 + c], pair_send.at[2], pair_recv.at[2], m, other)
    pair_sum.start()
    hear(heard_2, "yz")
    pass_on(heard_3, 2, "z")
    for copy in late_loads[1:]:
        copy.wait()

    for which in range(2):
        for xx, cc in group_x:
            arrived(part.at[which, c, x], recv_x.at[which, 2 * xx + cc])
        for cc in range(2):
            total = got_x[which, cc]
            for xx in range(1, nx):
                total = total + got_x[which, 2 * xx + cc]
            sum_x[(2 * cc + which) * share:(2 * cc + which + 1) * share, :] = total

    piece = 4 * share // ny
    own_piece = pl.ds(pl.multiple_of(y * piece, piece), piece)
    stage_y = []
    for yy in group_y:
        stage_y.append(remote(
            sum_x.at[pl.ds(pl.multiple_of(yy * piece, piece), piece)], got_y.at[y],
            send_y.at[yy], recv_y.at[y], at(x, z, yy), c))
        stage_y[-1].start()
    got_y[y] = sum_x[own_piece, :]

    for yy in group_y:
        arrived(sum_y, recv_y.at[yy])
    total = got_y[0]
    for yy in range(1, ny):
        total = total + got_y[yy]
    sum_y[...] = total

    hear(heard_3, "z")
    stage_z = []
    for zz in group_z:
        stage_z.append(remote(sum_y, got_z.at[z], send_z.at[zz], recv_z.at[z], at(x, zz, y), c))
        stage_z[-1].start()
    got_z[z] = total
    pair_grad.wait_recv()
    pair_sum.wait_recv()
    weights = jnp.concatenate([w_buf[0], w_buf[1]], axis=1)
    wide = 2 * SIDE

    def feature_part(low, high):
        for i in range(low, high):
            span = pl.ds(i * wide, wide)
            fgrad[span, :] = dot(weights, full_t[:, :, span].reshape(4 * SIDE, wide)).T

    feature_part(0, rows // wide)
    for copy in [pair_feat, pair_grad, pair_sum] + sums + stage_x[0] + stage_x[1] + stage_y:
        copy.wait_send()
    for zz in group_z:
        arrived(sum_y, recv_z.at[zz])
    total = got_z[0]
    for zz in range(1, nz):
        total = total + got_z[zz]
    every[x, own_piece, :] = total.astype(BF16)

    plane = [(i, j) for i in range(nx) for j in range(ny) if i or j]
    plane = [((x + i) % nx, (y + j) % ny) for i, j in sorted(plane, key=lambda p: -min(p[0], nx - p[0]) - min(p[1], ny - p[1]))]
    back = []
    for xx, yy in plane:
        back.append(remote(
            every.at[x, own_piece], every.at[x, own_piece], send_back.at[xx, yy], recv_back.at[x, y], at(xx, z, yy), c))
        back[-1].start()
    for copy in stage_z:
        copy.wait_send()
    for xx, yy in plane[::-1]:
        arrived(every.at[xx, pl.ds(pl.multiple_of(yy * piece, piece), piece)], recv_back.at[xx, yy])
    for which in range(2):
        for cc in range(2):
            base = (2 * cc + which) * share
            value = jnp.concatenate([every[q, base:base + share, :] for q in range(nx)], axis=0)
            wgrad[which, :, cc * SIDE:(cc + 1) * SIDE] = value.astype(F32).T

    for copy in back:
        copy.wait_send()


def write(feature_in, weight_in, feature_out, self_out, neighbor_out, sem):
    part = feature_in.shape[0] // 4
    copies = [
        pltpu.make_async_copy(feature_in.at[pl.ds(i * part, part)], feature_out.at[pl.ds(i * part, part)], sem.at[i])
        for i in range(4)
    ]
    copies += [
        pltpu.make_async_copy(weight_in.at[0], self_out, sem.at[4]),
        pltpu.make_async_copy(weight_in.at[1], neighbor_out, sem.at[5]),
    ]
    for copy in copies:
        copy.start()
    for copy in copies:
        copy.wait()


def body(torus, features, out_grad, block_tiles, block_cols, self_weight, neighbor_weight):
    nx, nz, ny = torus
    rows, columns = features.shape
    width = self_weight.shape[1]
    count = block_tiles.shape[0]
    share = SIDE // nx
    piece = 4 * share // ny
    dma = pltpu.SemaphoreType.DMA
    anywhere = pl.BlockSpec(memory_space=pl.ANY)
    heard = pltpu.SemaphoreType.REGULAR((3,))
    feature_grad, weight_grad = pl.pallas_call(
        functools.partial(kernel, torus),
        out_shape=(pltpu.VMEM((rows, columns), F32), pltpu.VMEM((2, columns, width), F32)),
        in_specs=[anywhere] * 6,
        out_specs=(pl.BlockSpec(memory_space=pltpu.VMEM),) * 2,
        scratch_shapes=[
            pltpu.VMEM((count, SIDE, SIDE), BF16),
            pltpu.VMEM((rows, 2 * SIDE), BF16),
            pltpu.VMEM((rows, columns), BF16),
            pltpu.VMEM((2, SIDE, width), BF16),
            pltpu.VMEM((1, count), jnp.int32),
            pltpu.VMEM((8, SIDE), jnp.int32),
            pltpu.SMEM((8, SIDE), jnp.int32),
            pltpu.VMEM((count + 1, SIDE, SIDE), F32),
            pltpu.VMEM((4, SIDE, rows), BF16),
            pltpu.VMEM((SIDE, rows), BF16),
            pltpu.VMEM((2 * HALO, SIDE, SIDE), BF16),
            pltpu.VMEM((2, HALO, SIDE, SIDE), BF16),
            pltpu.VMEM((2, HALO, SIDE, SIDE), BF16),
            pltpu.VMEM((2, 2, nx, share, SIDE), F32),
            pltpu.VMEM((2, 2 * nx, share, SIDE), F32),
            pltpu.VMEM((4 * share, SIDE), F32),
            pltpu.VMEM((ny, piece, SIDE), F32),
            pltpu.VMEM((piece, SIDE), F32),
            pltpu.VMEM((nz, piece, SIDE), F32),
            pltpu.VMEM((nx, 4 * share, SIDE), BF16),
            dma((12,)), dma((CHUNKS,)), dma((3,)), dma((3,)), dma((2,)), dma((2,)),
            heard, heard, heard,
            dma((2, 2 * nx)), dma((2, 2 * nx)), dma((ny,)), dma((ny,)), dma((nz,)), dma((nz,)),
            dma((nx, ny)), dma((nx, ny)),
        ],
        compiler_params=pltpu.CompilerParams(
            collective_id=0, has_side_effects=True, vmem_limit_bytes=VMEM_BYTES
        ),
        cost_estimate=pl.CostEstimate(flops=1100000000, bytes_accessed=4500000, transcendentals=0),
    )(features, out_grad, block_tiles, block_cols.reshape(1, count), self_weight, neighbor_weight)
    feature_grad = pltpu.with_memory_space_constraint(feature_grad, pltpu.VMEM)
    weight_grad = pltpu.with_memory_space_constraint(weight_grad, pltpu.VMEM)
    return pl.pallas_call(
        write,
        out_shape=(
            jax.ShapeDtypeStruct((rows, columns), F32),
            jax.ShapeDtypeStruct((columns, width), F32),
            jax.ShapeDtypeStruct((columns, width), F32),
        ),
        in_specs=[pl.BlockSpec(memory_space=pltpu.VMEM)] * 2,
        out_specs=(anywhere,) * 3,
        scratch_shapes=[dma((6,))],
        compiler_params=pltpu.CompilerParams(vmem_limit_bytes=VMEM_BYTES),
        cost_estimate=pl.CostEstimate(flops=0, bytes_accessed=2600000, transcendentals=0),
    )(feature_grad, weight_grad)


def solution(mesh):
    in_specs = (
        P("blk", "rep"),
        P("blk", "rep"),
        P("blk", None, None),
        P("blk"),
        P("rep", None),
        P("rep", None),
    )
    out_specs = (P("blk", "rep"), P("rep", None), P("rep", None))
    step = functools.partial(body, TORUS)
    return jax.shard_map(step, mesh=mesh, in_specs=in_specs, out_specs=out_specs, check_vma=False)
```

```python
import functools

import jax
import jax.numpy as jnp
from jax import lax
from jax.experimental import pallas as pl
from jax.experimental.pallas import tpu as pltpu
from jax.sharding import PartitionSpec as P

HALO = 2
SIDE = 128
TORUS = (4, 12, 8)
CHUNKS = 4
VMEM_BYTES = 60 * 1024 * 1024
BF16, F32 = jnp.bfloat16, jnp.float32


def dot(a, b):
    return jnp.dot(a, b, preferred_element_type=F32)


def kernel(
    torus,
    feat, grad, tiles, cols, self_w, neigh_w,
    fgrad, wgrad,
    tile_buf, feat_buf, grad_buf, w_buf, cols_v, index_v, index_s,
    chain, full_t, low_t, rim_tiles, rim_out, rim_in,
    part, got_x, sum_x, got_y, sum_y, got_z, every,
    load_sem, tile_sem, pair_send, pair_recv, rim_send, rim_recv,
    heard_1, heard_2, heard_3, send_x, recv_x, send_y, recv_y, send_z, recv_z, send_back, recv_back,
):
    nx, nz, ny = torus
    n = nx * nz * ny
    m, c = lax.axis_index("blk"), lax.axis_index("rep")
    x, z, y = m // (nz * ny), (m // ny) % nz, m % ny
    rows = grad.shape[0]
    blocks = rows // SIDE
    count = tiles.shape[0]
    per = count // blocks
    up, down = (m + 1) % n, (m + n - 1) % n
    other = 1 - c

    def at(xx, zz, yy):
        return (xx * nz + zz) * ny + yy

    def far_first(size):
        return sorted(range(1, size), key=lambda k: -min(k, size - k))

    group_x = [((x + k) % nx, (c + j) % 2) for k in far_first(nx) + [0] for j in ((0, 1) if k else (1,))]
    group_y = [(y + k) % ny for k in far_first(ny)]
    group_z = [(z + k) % nz for k in far_first(nz)]

    def remote(src, dst, send, recv, blk, rep):
        return pltpu.make_async_remote_copy(
            src_ref=src, dst_ref=dst, send_sem=send, recv_sem=recv,
            device_id={"blk": blk, "rep": rep}, device_id_type=pl.DeviceIdType.MESH,
        )

    def arrived(like, recv):
        pltpu.make_async_copy(like, like, recv).wait()

    def signal(sem, blk, rep):
        pl.semaphore_signal(sem, inc=1, device_id={"blk": blk, "rep": rep}, device_id_type=pl.DeviceIdType.MESH)

    barrier = pltpu.get_barrier_semaphore()
    near = [(up, c), (down, c)]
    near += [(at(x, (z + k) % nz, y), c) for k in (1, nz - 1)] + [(at(x, z, (y + k) % ny), c) for k in (1, ny - 1)]
    near += [(at((x + k) % nx, z, y), cc) for k in (1, nx - 1) for cc in (c, other)] + [(m, other)]
    for blk, rep in near:
        signal(barrier, blk, rep)

    def pass_on(sems, step, axes):
        for k in (step, -step):
            to = {"x": at((x + k + nx) % nx, z, y), "y": at(x, z, (y + k + ny) % ny), "z": at(x, (z + k + nz) % nz, y)}
            for i, axis in enumerate(axes):
                signal(sems.at[i], to[axis], c)

    def hear(sems, axes):
        for i in range(len(axes)):
            pl.semaphore_wait(sems.at[i], 2)

    own_cols = pl.ds(pl.multiple_of(c * SIDE, SIDE), SIDE)
    rim = HALO * SIDE
    ends = [k for k in range(HALO)] + [blocks - HALO + k for k in range(HALO)]
    rim_loads = [
        pltpu.make_async_copy(grad.at[pl.ds(0, rim)], grad_buf.at[pl.ds(0, rim)], load_sem.at[0]),
        pltpu.make_async_copy(grad.at[pl.ds(rows - rim, rim)], grad_buf.at[pl.ds(rows - rim, rim)], load_sem.at[1]),
    ]
    for k, b in enumerate(ends):
        rim_loads.append(pltpu.make_async_copy(tiles.at[b * per], rim_tiles.at[k], load_sem.at[2 + k]))
    load_cols = pltpu.make_async_copy(cols, cols_v, load_sem.at[6])
    load_grad = pltpu.make_async_copy(
        grad.at[pl.ds(rim, rows - 2 * rim)], grad_buf.at[pl.ds(rim, rows - 2 * rim)], load_sem.at[7])
    chunk = count // CHUNKS
    tile_loads = [
        pltpu.make_async_copy(tiles.at[pl.ds(i * chunk, chunk)], tile_buf.at[pl.ds(i * chunk, chunk)], tile_sem.at[i])
        for i in range(CHUNKS)
    ]
    late_loads = [
        pltpu.make_async_copy(feat, feat_buf.at[:, own_cols], load_sem.at[8]),
        pltpu.make_async_copy(self_w, w_buf.at[0], load_sem.at[9]),
        pltpu.make_async_copy(neigh_w, w_buf.at[1], load_sem.at[10]),
    ]
    for copy in [load_cols] + rim_loads + [load_grad] + tile_loads + late_loads:
        copy.start()

    load_cols.wait()
    slot = cols_v[...] - m * blocks
    slot = jnp.concatenate([slot, jnp.full((1, SIDE - count), -1, jnp.int32)], axis=1)
    across = jnp.broadcast_to(slot, (SIDE, SIDE))
    along = across.T
    row = lax.broadcasted_iota(jnp.int32, (SIDE, SIDE), 0)
    lane = lax.broadcasted_iota(jnp.int32, (SIDE, SIDE), 1)
    before = jnp.max(jnp.where((across == along) & (row < lane), row, -1), axis=0, keepdims=True)
    final = jnp.max(jnp.where((along == lane) & (row < count), row, -1), axis=0, keepdims=True)
    index_v[0:1, :] = jnp.where(before < 0, count, before)
    index_v[1:2, :] = jnp.where(final < 0, count, final)
    to_scalar = pltpu.make_async_copy(index_v, index_s, load_sem.at[11])
    to_scalar.start()
    chain[count] = jnp.zeros((SIDE, SIDE), F32)

    for copy in rim_loads:
        copy.wait()
    for k, b in enumerate(ends):
        rim_out[k // HALO, k % HALO] = dot(grad_buf[b * SIDE:(b + 1) * SIDE, :].T, rim_tiles[k]).astype(BF16)

    pl.semaphore_wait(barrier, len(near))
    sums = [
        remote(rim_out.at[0], rim_in.at[0], rim_send.at[0], rim_recv.at[0], down, c),
        remote(rim_out.at[1], rim_in.at[1], rim_send.at[1], rim_recv.at[1], up, c),
    ]
    for copy in sums:
        copy.start()
    pair_feat = remote(feat, feat_buf.at[:, own_cols], pair_send.at[0], pair_recv.at[0], m, other)
    pair_feat.start()
    pass_on(heard_1, 1, "xyz")
    to_scalar.wait()
    load_grad.wait()

    for b in range(blocks):
        span = pl.ds(b * SIDE, SIDE)
        full_t[c, :, span] = grad_buf[span, :].T

    def tile_work(i):
        tile_loads[i].wait()
        for b in range(i * blocks // CHUNKS, (i + 1) * blocks // CHUNKS):
            product = dot(
                full_t[c, :, pl.ds(b * SIDE, SIDE)],
                jnp.concatenate([tile_buf[b * per + k] for k in range(per)], axis=1))
            for k in range(per):
                t = b * per + k
                chain[t] = chain[index_s[0, t]] + product[:, k * SIDE:(k + 1) * SIDE]

    for i in range(CHUNKS // 2):
        tile_work(i)

    share = SIDE // nx
    stage_x = [[], []]

    def send_share(which, value):
        for r in range(2):
            for q in range(nx):
                part[which, r, q] = value[q * share:(q + 1) * share, r * SIDE:(r + 1) * SIDE]
        for xx, cc in group_x:
            stage_x[which].append(remote(
                part.at[which, cc, xx], got_x.at[which, 2 * x + c],
                send_x.at[which, 2 * xx + cc], recv_x.at[which, 2 * x + c], at(xx, z, y), cc))
            stage_x[which][-1].start()
        got_x[which, 2 * x + c] = part[which, c, x]

    late_loads[0].wait()
    pair_feat.wait_recv()
    hear(heard_1, "xyz")
    pass_on(heard_2, 2, "yz")
    send_share(0, dot(full_t[c], feat_buf[...]))
    pair_grad = remote(full_t.at[c], full_t.at[c], pair_send.at[1], pair_recv.at[1], m, other)
    pair_grad.start()
    for i in range(CHUNKS // 2, CHUNKS):
        tile_work(i)

    def column_block(b, value):
        span = pl.ds(b * SIDE, SIDE)
        hi = value.astype(BF16)
        full_t[2 + c, :, span] = hi
        low_t[:, span] = (value - hi.astype(F32)).astype(BF16)

    for b in range(HALO, blocks - HALO):
        column_block(b, chain[index_s[1, b]])

    def product(*spans):
        spans = [pl.ds(low, high - low) for low, high in spans]
        right = jnp.concatenate([feat_buf[span, :] for span in spans], axis=0)
        high_part = jnp.concatenate([full_t[2 + c, :, span] for span in spans], axis=1)
        low_part = jnp.concatenate([low_t[:, span] for span in spans], axis=1)
        return dot(high_part, right) + dot(low_part, right)

    inner = product((rim, rows - rim))
    for copy in sums:
        copy.wait_recv()
    for k in range(HALO):
        b = blocks - 1 - k
        column_block(b, chain[index_s[1, b]] + rim_in[0, k].astype(F32))
        b = HALO - 1 - k
        column_block(b, chain[index_s[1, b]] + rim_in[1, k].astype(F32))
    send_share(1, inner + product((0, rim), (rows - rim, rows)))
    hear(heard_2, "yz")
    pass_on(heard_3, 2, "z")
    for copy in late_loads[1:]:
        copy.wait()

    for which in range(2):
        for xx, cc in group_x:
            arrived(part.at[which, c, x], recv_x.at[which, 2 * xx + cc])
        for cc in range(2):
            total = got_x[which, cc]
            for xx in range(1, nx):
                total = total + got_x[which, 2 * xx + cc]
            sum_x[(2 * cc + which) * share:(2 * cc + which + 1) * share, :] = total

    piece = 4 * share // ny
    own_piece = pl.ds(pl.multiple_of(y * piece, piece), piece)
    stage_y = []
    for yy in group_y:
        stage_y.append(remote(
            sum_x.at[pl.ds(pl.multiple_of(yy * piece, piece), piece)], got_y.at[y],
            send_y.at[yy], recv_y.at[y], at(x, z, yy), c))
        stage_y[-1].start()
    pair_sum = remote(full_t.at[2 + c], full_t.at[2 + c], pair_send.at[2], pair_recv.at[2], m, other)
    pair_sum.start()
    got_y[y] = sum_x[own_piece, :]

    for yy in group_y:
        arrived(sum_y, recv_y.at[yy])
    total = got_y[0]
    for yy in range(1, ny):
        total = total + got_y[yy]
    sum_y[...] = total

    hear(heard_3, "z")
    stage_z = []
    for zz in group_z:
        stage_z.append(remote(sum_y, got_z.at[z], send_z.at[zz], recv_z.at[z], at(x, zz, y), c))
        stage_z[-1].start()
    got_z[z] = total
    pair_grad.wait_recv()
    pair_sum.wait_recv()
    weights = jnp.concatenate([w_buf[0], w_buf[1]], axis=1)
    wide = 2 * SIDE

    def feature_part(low, high):
        for i in range(low, high):
            span = pl.ds(i * wide, wide)
            fgrad[span, :] = dot(weights, full_t[:, :, span].reshape(4 * SIDE, wide)).T

    feature_part(0, rows // wide)
    for copy in [pair_feat, pair_grad, pair_sum] + sums + stage_x[0] + stage_x[1] + stage_y:
        copy.wait_send()
    for zz in group_z:
        arrived(sum_y, recv_z.at[zz])
    total = got_z[0]
    for zz in range(1, nz):
        total = total + got_z[zz]
    every[x, own_piece, :] = total.astype(BF16)

    plane = [(i, j) for i in range(nx) for j in range(ny) if i or j]
    plane = [((x + i) % nx, (y + j) % ny) for i, j in sorted(plane, key=lambda p: -min(p[0], nx - p[0]) - min(p[1], ny - p[1]))]
    back = []
    for xx, yy in plane:
        back.append(remote(
            every.at[x, own_piece], every.at[x, own_piece], send_back.at[xx, yy], recv_back.at[x, y], at(xx, z, yy), c))
        back[-1].start()
    for copy in stage_z:
        copy.wait_send()
    for xx, yy in plane[::-1]:
        arrived(every.at[xx, pl.ds(pl.multiple_of(yy * piece, piece), piece)], recv_back.at[xx, yy])
    for which in range(2):
        for cc in range(2):
            base = (2 * cc + which) * share
            value = jnp.concatenate([every[q, base:base + share, :] for q in range(nx)], axis=0)
            wgrad[which, :, cc * SIDE:(cc + 1) * SIDE] = value.astype(F32).T

    for copy in back:
        copy.wait_send()


def write(feature_in, weight_in, feature_out, self_out, neighbor_out, sem):
    part = feature_in.shape[0] // 4
    copies = [
        pltpu.make_async_copy(feature_in.at[pl.ds(i * part, part)], feature_out.at[pl.ds(i * part, part)], sem.at[i])
        for i in range(4)
    ]
    copies += [
        pltpu.make_async_copy(weight_in.at[0], self_out, sem.at[4]),
        pltpu.make_async_copy(weight_in.at[1], neighbor_out, sem.at[5]),
    ]
    for copy in copies:
        copy.start()
    for copy in copies:
        copy.wait()


def body(torus, features, out_grad, block_tiles, block_cols, self_weight, neighbor_weight):
    nx, nz, ny = torus
    rows, columns = features.shape
    width = self_weight.shape[1]
    count = block_tiles.shape[0]
    share = SIDE // nx
    piece = 4 * share // ny
    dma = pltpu.SemaphoreType.DMA
    anywhere = pl.BlockSpec(memory_space=pl.ANY)
    heard = pltpu.SemaphoreType.REGULAR((3,))
    feature_grad, weight_grad = pl.pallas_call(
        functools.partial(kernel, torus),
        out_shape=(pltpu.VMEM((rows, columns), F32), pltpu.VMEM((2, columns, width), F32)),
        in_specs=[anywhere] * 6,
        out_specs=(pl.BlockSpec(memory_space=pltpu.VMEM),) * 2,
        scratch_shapes=[
            pltpu.VMEM((count, SIDE, SIDE), BF16),
            pltpu.VMEM((rows, 2 * SIDE), BF16),
            pltpu.VMEM((rows, columns), BF16),
            pltpu.VMEM((2, SIDE, width), BF16),
            pltpu.VMEM((1, count), jnp.int32),
            pltpu.VMEM((8, SIDE), jnp.int32),
            pltpu.SMEM((8, SIDE), jnp.int32),
            pltpu.VMEM((count + 1, SIDE, SIDE), F32),
            pltpu.VMEM((4, SIDE, rows), BF16),
            pltpu.VMEM((SIDE, rows), BF16),
            pltpu.VMEM((2 * HALO, SIDE, SIDE), BF16),
            pltpu.VMEM((2, HALO, SIDE, SIDE), BF16),
            pltpu.VMEM((2, HALO, SIDE, SIDE), BF16),
            pltpu.VMEM((2, 2, nx, share, SIDE), F32),
            pltpu.VMEM((2, 2 * nx, share, SIDE), F32),
            pltpu.VMEM((4 * share, SIDE), F32),
            pltpu.VMEM((ny, piece, SIDE), F32),
            pltpu.VMEM((piece, SIDE), F32),
            pltpu.VMEM((nz, piece, SIDE), F32),
            pltpu.VMEM((nx, 4 * share, SIDE), BF16),
            dma((12,)), dma((CHUNKS,)), dma((3,)), dma((3,)), dma((2,)), dma((2,)),
            heard, heard, heard,
            dma((2, 2 * nx)), dma((2, 2 * nx)), dma((ny,)), dma((ny,)), dma((nz,)), dma((nz,)),
            dma((nx, ny)), dma((nx, ny)),
        ],
        compiler_params=pltpu.CompilerParams(
            collective_id=0, has_side_effects=True, vmem_limit_bytes=VMEM_BYTES
        ),
        cost_estimate=pl.CostEstimate(flops=1100000000, bytes_accessed=4500000, transcendentals=0),
    )(features, out_grad, block_tiles, block_cols.reshape(1, count), self_weight, neighbor_weight)
    feature_grad = pltpu.with_memory_space_constraint(feature_grad, pltpu.VMEM)
    weight_grad = pltpu.with_memory_space_constraint(weight_grad, pltpu.VMEM)
    return pl.pallas_call(
        write,
        out_shape=(
            jax.ShapeDtypeStruct((rows, columns), F32),
            jax.ShapeDtypeStruct((columns, width), F32),
            jax.ShapeDtypeStruct((columns, width), F32),
        ),
        in_specs=[pl.BlockSpec(memory_space=pltpu.VMEM)] * 2,
        out_specs=(anywhere,) * 3,
        scratch_shapes=[dma((6,))],
        compiler_params=pltpu.CompilerParams(vmem_limit_bytes=VMEM_BYTES),
        cost_estimate=pl.CostEstimate(flops=0, bytes_accessed=2600000, transcendentals=0),
    )(feature_grad, weight_grad)


def solution(mesh):
    in_specs = (
        P("blk", "rep"),
        P("blk", "rep"),
        P("blk", None, None),
        P("blk"),
        P("rep", None),
        P("rep", None),
    )
    out_specs = (P("blk", "rep"), P("rep", None), P("rep", None))
    step = functools.partial(body, TORUS)
    return jax.shard_map(step, mesh=mesh, in_specs=in_specs, out_specs=out_specs, check_vma=False)
```
